32 devices in a mesh: group: 2 (over x), seq: 16 (over z, y, core).
Axes of the slice: x: 2, y: 2, z: 4, core: 2. Of those that a mesh axis runs over, the one named last changes fastest.
Arguments:
- queries: bfloat16 [96, 128, 2560], P(('group', 'seq')), parts along dimension 0, may hold values from -9 to 9
- keys: bfloat16 [96, 128, 2560], P(('group', 'seq')), parts along dimension 0, may hold values from -9 to 9
- values: bfloat16 [96, 128, 2560], P(('group', 'seq')), parts along dimension 0, may hold values from -6 to 6
- block_list: int32 [96, 20, 2], P('group'), parts along dimension 0, may hold values from 0 to 47, as said below
- list_len: int32 [96, 20], P('group'), parts along dimension 0, may hold values from 0 to 2, as said below
- window_time: int32 [20], replicated, may hold values from 0 to 1
- window_rows: int32 [20], replicated, may hold values from 0 to 1
Outputs:
- attention_out: bfloat16 [96, 128, 2560], P(('group', 'seq')), parts along dimension 0
The draws below stay inside these ranges and needn't reach their ends.
There are 2 independent parts, one for each index of `group`. The reference program is written for one: setup_inputs(seed, part) draws one part's arguments, and reference() takes and returns one part's arrays. A program takes and returns all parts, laid end to end along the dimension named above; an argument that names none is the same for every part. Nothing has to cross between parts.
Inputs may be any that keep to these rules, and one draw needn't show every extreme that they name: `block_list`: for the 3 query tiles of one block and one head, all listed tiles lie on a single other block, and together the used entries name exactly 2 distinct tiles; one list's entries are distinct. For the query tiles of one block, no other block holds listed tiles of more than 2 heads, and some block holds those of exactly 2 heads, so the distinct listed pairs of tile and head of one block on another block number at most 4, reached in every draw. Entries of block_list at and after position list_len are not used.
All inputs are finite; a program needn't handle non-finite values.
Results may differ from the reference program's by a relative error of at most 0.0032.
Values may be sent and summed in bfloat16 or wider, within the bound.
A program may use at most 128 MiB of HBM per device.

```python
import math
import jax
import jax.numpy as jnp
from jax import lax

HEADS = 20
HEAD_DIM = 128
FEAT = 2560
TILE_TOK = 128
TIME_TILES = 1
ROW_TILES = 3
ROW_BLOCKS = 2
LIST = 2
BLOCKS = 16
TILES_DEV = 3
TILES = 48
HEADS_SRC = 2


def draw_queries(key, part):
    inner = jax.random.fold_in(key, 11)
    field = 1.5 * jax.random.truncated_normal(inner, -6.0, 6.0, (TILES, TILE_TOK, FEAT), jnp.float32)
    return field.astype(jnp.bfloat16)


def draw_keys(key, part):
    inner = jax.random.fold_in(key, 13)
    field = 1.5 * jax.random.truncated_normal(inner, -6.0, 6.0, (TILES, TILE_TOK, FEAT), jnp.float32)
    return field.astype(jnp.bfloat16)


def make_lists(key):
    inner = jax.random.fold_in(key, 23)
    keys_all = jax.random.split(inner, 7)
    blocks = jnp.arange(BLOCKS)
    special = jax.random.randint(keys_all[6], (), 0, BLOCKS)
    before = (special + BLOCKS - 1) % BLOCKS
    is_self = blocks[:, None] == blocks[None, :]
    favoured = (blocks[:, None] == special) & (blocks[None, :] == before)
    ranks = jax.vmap(lambda sub: jax.random.permutation(sub, BLOCKS))(jax.random.split(keys_all[0], BLOCKS))
    ranking = jnp.where(is_self, 2 * BLOCKS, 0) + jnp.where(favoured, -BLOCKS, 0) + ranks
    order = jnp.argsort(ranking, axis=1, stable=True)
    group = jnp.arange(HEADS) // HEADS_SRC
    source = order[:, group]
    first = jax.random.randint(keys_all[1], (BLOCKS, HEADS), 0, TILES_DEV)
    stride = jax.random.randint(keys_all[2], (BLOCKS, HEADS), 1, TILES_DEV)
    second = (first + stride) % TILES_DEV
    full_tile = jax.random.randint(keys_all[3], (BLOCKS, HEADS), 0, TILES_DEV)
    lengths = jax.random.randint(keys_all[4], (BLOCKS, TILES_DEV, HEADS), 0, LIST + 1)
    lengths = jnp.where(jnp.arange(TILES_DEV)[None, :, None] == full_tile[:, None, :], LIST, lengths)
    flip = jax.random.randint(keys_all[5], (BLOCKS, TILES_DEV, HEADS), 0, 2)
    one_tile = (source * TILES_DEV + first)[:, None, :]
    other_tile = (source * TILES_DEV + second)[:, None, :]
    entry_first = jnp.where(flip == 1, other_tile, one_tile)
    entry_second = jnp.where(flip == 1, one_tile, other_tile)
    listed = jnp.stack([entry_first, entry_second], axis=-1).reshape(TILES, HEADS, LIST)
    return (listed.astype(jnp.int32), lengths.reshape(TILES, HEADS).astype(jnp.int32))


def draw_block_list(key, part):
    return make_lists(key)[0]


def draw_list_len(key, part):
    return make_lists(key)[1]


def with_ends(values, stream_key, smallest, largest):
    longest = values.shape.index(max(values.shape))
    spots = []
    for shift in (0, 1):
        where = [jax.random.randint(jax.random.fold_in(stream_key, axis), (), 0, length) for axis, length in enumerate(values.shape)]
        where[longest] = (where[longest] + shift) % values.shape[longest]
        spots.append(tuple(where))
    return values.at[spots[0]].set(smallest).at[spots[1]].set(largest)


def block_levels(own_key, shape, pieces, least, high):
    gain, own = 1.0, jax.random.fold_in(own_key, 6)
    for axis_at, blocks in pieces:
        steps = jnp.exp(jax.random.uniform(jax.random.fold_in(own, axis_at), (blocks,), jnp.float32, least / len(pieces), high / len(pieces)))
        gain = gain * jnp.repeat(steps, shape[axis_at] // blocks).reshape([-1 if axis == axis_at else 1 for axis in range(len(shape))])
    return gain


def scatter_about(stream_key, extent, deviation, limit, cuts=(), kind=jnp.bfloat16):
    entries = deviation * jax.random.normal(stream_key, extent, jnp.float32)
    if cuts:
        entries = entries * block_levels(stream_key, extent, cuts, -0.22, 0.18)
    return jnp.clip(entries, -limit, limit).astype(kind)


def setup_inputs(seed: int = 0, part: int = 0) -> dict:
    seeds = jax.random.split(jax.random.key(seed), 8)
    part_splits = jax.random.split(jax.random.fold_in(seeds[7], part), 8)
    return {
        "queries": draw_queries(jax.random.fold_in(jax.random.fold_in(seeds[7], part), 71), part),
        "keys": draw_keys(jax.random.fold_in(jax.random.fold_in(seeds[7], part), 71), part),
        "values": scatter_about(part_splits[2], (TILES, TILE_TOK, FEAT), 1.0, 6.0, ((0, 16),)),
        "block_list": draw_block_list(jax.random.fold_in(jax.random.fold_in(seeds[7], part), 71), part),
        "list_len": draw_list_len(jax.random.fold_in(jax.random.fold_in(seeds[7], part), 71), part),
        "window_time": with_ends(jax.random.randint(seeds[5], (HEADS,), 0, 2), jax.random.fold_in(seeds[5], 1), 0, 1).astype(jnp.int32),
        "window_rows": with_ends(jax.random.randint(seeds[6], (HEADS,), 0, 2), jax.random.fold_in(seeds[6], 1), 0, 1).astype(jnp.int32),
    }


BIG_NEG = -1e+30

def tile_coords(ids):
    block = ids // TILES_DEV
    local = ids % TILES_DEV
    time_pos = block // ROW_BLOCKS * TIME_TILES + local // ROW_TILES
    row_pos = block % ROW_BLOCKS * ROW_TILES + local % ROW_TILES
    return (time_pos, row_pos)

def tile_number(time_pos, row_pos):
    block = time_pos // TIME_TILES * ROW_BLOCKS + row_pos // ROW_TILES
    local = time_pos % TIME_TILES * ROW_TILES + row_pos % ROW_TILES
    return (block * TILES_DEV + local).astype(jnp.int32)

def reference(queries, keys, values, block_list, list_len, window_time, window_rows):
    time_count = TIME_TILES * BLOCKS // ROW_BLOCKS
    row_count = ROW_BLOCKS * ROW_TILES
    ids = jnp.arange(TILES, dtype=jnp.int32)
    time_pos, row_pos = tile_coords(ids)
    step_time = jnp.array([-1, -1, -1, 0, 0, 0, 1, 1, 1], jnp.int32)
    step_row = jnp.array([-1, 0, 1, -1, 0, 1, -1, 0, 1], jnp.int32)
    near_time = time_pos[:, None] + step_time[None, :]
    near_row = row_pos[:, None] + step_row[None, :]
    inside = (near_time >= 0) & (near_time < time_count) & (near_row >= 0) & (near_row < row_count)
    near_ids = tile_number(jnp.clip(near_time, 0, time_count - 1), jnp.clip(near_row, 0, row_count - 1))
    live = jnp.arange(LIST, dtype=jnp.int32)[None, None, :] < list_len[:, :, None]
    scale = 1.0 / math.sqrt(HEAD_DIM)

    def one_head(head):
        q_head = lax.dynamic_slice_in_dim(queries, head * HEAD_DIM, HEAD_DIM, 2)
        k_head = lax.dynamic_slice_in_dim(keys, head * HEAD_DIM, HEAD_DIM, 2)
        v_head = lax.dynamic_slice_in_dim(values, head * HEAD_DIM, HEAD_DIM, 2)
        far_ids = lax.dynamic_index_in_dim(block_list, head, 1, keepdims=False)
        key_rows = jnp.concatenate([k_head[near_ids].reshape(TILES, 9 * TILE_TOK, HEAD_DIM), k_head[far_ids].reshape(TILES, LIST * TILE_TOK, HEAD_DIM)], axis=1)
        value_rows = jnp.concatenate([v_head[near_ids].reshape(TILES, 9 * TILE_TOK, HEAD_DIM), v_head[far_ids].reshape(TILES, LIST * TILE_TOK, HEAD_DIM)], axis=1)
        scores = jnp.einsum('txd,tyd->txy', q_head.astype(jnp.float32), key_rows.astype(jnp.float32)) * scale
        win_ok = inside & (jnp.abs(step_time)[None, :] <= window_time[head]) & (jnp.abs(step_row)[None, :] <= window_rows[head])
        list_ok = lax.dynamic_index_in_dim(live, head, 1, keepdims=False)
        usable = jnp.concatenate([jnp.repeat(win_ok, TILE_TOK, axis=1), jnp.repeat(list_ok, TILE_TOK, axis=1)], axis=1)
        scores = jnp.where(usable[:, None, :], scores, BIG_NEG)
        top = lax.optimization_barrier(jnp.max(scores, axis=2, keepdims=True))
        weights = jnp.exp(scores - top)
        total = lax.optimization_barrier(jnp.sum(weights, axis=2, keepdims=True))
        rounded = lax.optimization_barrier(weights.astype(jnp.bfloat16))
        mixed = jnp.einsum('txy,tyd->txd', rounded.astype(jnp.float32), value_rows.astype(jnp.float32))
        return (mixed / total).astype(jnp.bfloat16)
    results = lax.map(one_head, jnp.arange(HEADS, dtype=jnp.int32))
    return jnp.transpose(results, (1, 2, 0, 3)).reshape(TILES, TILE_TOK, FEAT)
```

```python
import functools
import math

import jax
import jax.numpy as jnp
from jax import lax
from jax.experimental import pallas as pl
from jax.experimental.pallas import tpu as pltpu
from jax.sharding import PartitionSpec as P

ROW_TILES = 3
ROW_BLOCKS = 2
LIST = 2
CHUNK_HEADS = 4
BIG_NEG = -1e30


def kernel(
    blocks, heads, tok, dim, per_source,
    send_meta, recv_meta, biases, q_hbm, k_hbm, v_hbm, out_ref,
    qs, kv, edge, near, near_edge, relayed, relayed_edge, far_out, far_in, acc, top, total,
    load_sem, edge_sem, near_sem, near_edge_sem, relay_sem, relay_edge_sem, far_sem,
):
    me = lax.axis_index("seq")
    side = lax.rem(me, ROW_BLOCKS)
    time = me // ROW_BLOCKS
    times = blocks // ROW_BLOCKS
    odd = lax.rem(time, 2)
    partner = me + 1 - 2 * side
    mirror = me + ROW_BLOCKS * (1 - 2 * odd)
    ahead = 2 * (1 - 2 * odd)
    gives = jnp.logical_and(time + ahead >= 0, time + ahead < times)
    takes = jnp.logical_and(time - ahead >= 0, time - ahead < times)
    relay_to = me + ROW_BLOCKS * ahead
    edge_tile = 2 - 2 * side
    other_tile = 2 * side
    chunks = heads // CHUNK_HEADS

    def remote(src, dst, sems, device):
        return pltpu.make_async_remote_copy(
            src_ref=src, dst_ref=dst, send_sem=sems.at[0], recv_sem=sems.at[1],
            device_id={"seq": device}, device_id_type=pl.DeviceIdType.MESH,
        )

    def part_of(chunk):
        return pl.ds(chunk * CHUNK_HEADS, CHUNK_HEADS)

    def near_copy(chunk):
        part = part_of(chunk)
        return remote(kv.at[:, part], near.at[:, part], near_sem.at[chunk], mirror)

    def near_edge_copy(chunk):
        part = part_of(chunk)
        return remote(
            near.at[:, part, edge_tile], near_edge.at[:, part],
            near_edge_sem.at[chunk], partner,
        )

    def relay_copy(chunk):
        part = part_of(chunk)
        return remote(
            near.at[:, part], relayed.at[:, part], relay_sem.at[chunk], relay_to
        )

    def relay_edge_copy(chunk):
        part = part_of(chunk)
        return remote(
            relayed.at[:, part, edge_tile], relayed_edge.at[:, part],
            relay_edge_sem.at[chunk], partner,
        )

    def far_copy(offset):
        return remote(
            far_out.at[offset], far_in.at[offset], far_sem.at[offset], lax.rem(me + offset, blocks)
        )

    def loads(head):
        cols = pl.ds(pl.multiple_of(head * dim, dim), dim)
        return [
            pltpu.make_async_copy(array.at[:, :, cols], held, load_sem.at[which, head])
            for which, (array, held) in enumerate(
                ((k_hbm, kv.at[0, head]), (v_hbm, kv.at[1, head]), (q_hbm, qs.at[head]))
            )
        ]

    def start_loads(head, carry):
        for copy in loads(head):
            copy.start()
        return carry

    def end_loads(head, carry):
        for copy in loads(head):
            copy.wait()
        return carry

    lax.fori_loop(0, heads, start_loads, 0)
    barrier = pltpu.get_barrier_semaphore()

    def greet(offset, carry):
        pl.semaphore_signal(
            barrier, inc=1, device_id={"seq": lax.rem(me + offset, blocks)},
            device_id_type=pl.DeviceIdType.MESH,
        )
        return carry

    lax.fori_loop(1, blocks, greet, 0)
    lax.fori_loop(0, heads, end_loads, 0)
    pl.semaphore_wait(barrier, blocks - 1)

    edge_copy = remote(kv.at[:, :, edge_tile], edge, edge_sem, partner)
    edge_copy.start()

    def start_near(chunk, carry):
        near_copy(chunk).start()
        return carry

    lax.fori_loop(0, chunks, start_near, 0)

    def start_far(offset, carry):
        target = lax.rem(me + offset, blocks)
        for pair in range(per_source):
            head = send_meta[target, 3 * pair]
            for which in range(LIST):
                tile = send_meta[target, 3 * pair + 1 + which]
                for part in range(2):
                    far_out[offset, pair * LIST + which, part] = kv[part, head, tile]
        far_copy(offset).start()
        return carry

    lax.fori_loop(1, blocks, start_far, 0)

    factor = math.log2(math.e) / math.sqrt(dim)

    def scores_of(query, key, bias):
        product = lax.dot_general(
            query, key, (((1,), (1,)), ((), ())), preferred_element_type=jnp.float32
        )
        return product * factor + bias

    def fold(head, tile, scores, value, first):
        high = jnp.max(scores, axis=1, keepdims=True)
        if not first:
            old = top[head, tile]
            high = jnp.maximum(high, old)
            shrink = jnp.exp2(old - high)
        weights = jnp.exp2(scores - high)
        amount = jnp.sum(weights, axis=1, keepdims=True)
        mixed = jnp.dot(
            weights.astype(jnp.bfloat16), value, preferred_element_type=jnp.float32
        )
        if not first:
            amount = amount + total[head, tile] * shrink
            mixed = mixed + acc[head, tile] * shrink
        return high, amount, mixed

    def keep(head, tile, state):
        top[head, tile], total[head, tile], acc[head, tile] = state

    def window_row(head, rows, edges, own):
        along = jnp.float32(0.0) if own else biases[0, head]
        lane = lax.broadcasted_iota(jnp.int32, (1, 3 * tok), 1)
        bias = jnp.where(lane < tok, along, biases[1 if own else 2, head])
        k_mid, v_mid = rows[0, head, 1], rows[1, head, 1]
        k_edge, v_edge = rows[0, head, edge_tile], rows[1, head, edge_tile]
        k_other, v_other = rows[0, head, other_tile], rows[1, head, other_tile]
        k_out, v_out = edges[0, head], edges[1, head]
        for tile, key, value in (
            (1, (k_mid, k_edge, k_other), (v_mid, v_edge, v_other)),
            (edge_tile, (k_edge, k_mid, k_out), (v_edge, v_mid, v_out)),
            (other_tile, (k_other, k_mid), (v_other, v_mid)),
        ):
            key = jnp.concatenate(key, axis=0)
            value = jnp.concatenate(value, axis=0)
            scores = scores_of(qs[head, tile], key, bias[:, : key.shape[0]])
            keep(head, tile, fold(head, tile, scores, value, own))

    edge_copy.wait_recv()

    def own_row(head, carry):
        window_row(head, kv, edge, True)
        return carry

    lax.fori_loop(0, heads, own_row, 0)

    def near_rows(chunk):
        def step(inner, carry):
            window_row(chunk * CHUNK_HEADS + inner, near, near_edge, False)
            return carry

        lax.fori_loop(0, CHUNK_HEADS, step, 0)

    def relayed_rows(chunk):
        def step(inner, carry):
            window_row(chunk * CHUNK_HEADS + inner, relayed, relayed_edge, False)
            return carry

        lax.fori_loop(0, CHUNK_HEADS, step, 0)

    def relay_arrived(chunk):
        relay_copy(chunk).wait_recv()
        relay_edge_copy(chunk).start()

    def relay_used(chunk):
        relay_edge_copy(chunk).wait_recv()
        relayed_rows(chunk)

    def time_chunk(chunk, carry):
        near_copy(chunk).wait_recv()
        near_edge_copy(chunk).start()

        @pl.when(gives)
        def _():
            relay_copy(chunk).start()

        @pl.when(jnp.logical_and(takes, chunk > 0))
        def _():
            relay_arrived(chunk - 1)

        near_edge_copy(chunk).wait_recv()
        near_rows(chunk)

        @pl.when(jnp.logical_and(takes, chunk > 0))
        def _():
            relay_used(chunk - 1)

        return carry

    lax.fori_loop(0, chunks, time_chunk, 0)

    @pl.when(takes)
    def _():
        relay_arrived(chunks - 1)
        relay_used(chunks - 1)

    def far_arrived(offset, carry):
        far_copy(offset).wait_recv()
        return carry

    lax.fori_loop(1, blocks, far_arrived, 0)

    def far_head(head, carry):
        cols = pl.ds(pl.multiple_of(head * dim, dim), dim)
        offset, slot = recv_meta[0, head], recv_meta[1, head]
        key = jnp.concatenate([far_in[offset, slot + w, 0] for w in range(LIST)], axis=0)
        value = jnp.concatenate([far_in[offset, slot + w, 1] for w in range(LIST)], axis=0)
        lane = lax.broadcasted_iota(jnp.int32, (1, LIST * tok), 1)
        for tile in range(ROW_TILES):
            bias = jnp.where(lane < tok, biases[3 + 2 * tile, head], biases[4 + 2 * tile, head])
            scores = scores_of(qs[head, tile], key, bias)
            _, amount, mixed = fold(head, tile, scores, value, False)
            out_ref[tile, :, cols] = (mixed / amount).astype(out_ref.dtype)
        return carry

    lax.fori_loop(0, heads, far_head, 0)

    edge_copy.wait_send()

    def sent(chunk, carry):
        near_copy(chunk).wait_send()
        near_edge_copy(chunk).wait_send()

        @pl.when(gives)
        def _():
            relay_copy(chunk).wait_send()

        @pl.when(takes)
        def _():
            relay_edge_copy(chunk).wait_send()

        return carry

    lax.fori_loop(0, chunks, sent, 0)

    def far_sent(offset, carry):
        far_copy(offset).wait_send()
        return carry

    lax.fori_loop(1, blocks, far_sent, 0)


def listed(block_list, list_len, window_time, window_rows, blocks, heads, per_source):
    me = lax.axis_index("seq")
    lists = block_list.reshape(blocks, ROW_TILES, heads, LIST)
    lens = list_len.reshape(blocks, ROW_TILES, heads, 1)
    live = jnp.arange(LIST, dtype=jnp.int32) < lens
    low = jnp.min(jnp.where(live, lists, jnp.int32(1 << 20)), axis=(1, 3))
    high = jnp.max(jnp.where(live, lists, jnp.int32(-1)), axis=(1, 3))
    source = low // ROW_TILES
    low_tile, high_tile = low % ROW_TILES, high % ROW_TILES
    number = jnp.arange(heads, dtype=jnp.int32)[None, :]
    mine = source == me
    first = jnp.min(jnp.where(mine, number, heads), axis=1, keepdims=True)
    first = jnp.where(first == heads, 0, first)
    last = jnp.max(jnp.where(mine, number, 0), axis=1, keepdims=True)
    columns = []
    for pick in (first, last)[:per_source]:
        hit = number == pick
        columns += [
            pick[:, 0],
            jnp.sum(jnp.where(hit, low_tile, 0), axis=1),
            jnp.sum(jnp.where(hit, high_tile, 0), axis=1),
        ]
    send_meta = jnp.stack(columns, axis=1)

    def own(table):
        return lax.dynamic_index_in_dim(table, me, 0, keepdims=False)

    own_source, own_low, own_high = own(source), own(low), own(high)
    own_lists, own_live = own(lists), own(live)
    earlier = (own_source[None, :] == own_source[:, None]) & (number < number.T)
    rank = jnp.minimum(jnp.any(earlier, axis=1).astype(jnp.int32), per_source - 1)
    recv_meta = jnp.stack([(me - own_source + blocks) % blocks, LIST * rank], axis=0)
    in_time, in_rows = window_time > 0, window_rows > 0
    rows = [in_time, in_rows, in_time & in_rows]
    for tile in range(ROW_TILES):
        for wanted in (own_low, own_high):
            found = own_live[tile] & (own_lists[tile] == wanted[:, None])
            rows.append(jnp.any(found, axis=1))
    biases = jnp.where(jnp.stack(rows, axis=0), 0.0, BIG_NEG).astype(jnp.float32)
    return send_meta, recv_meta, biases


def on_device(queries, keys, values, block_list, list_len, window_time, window_rows):
    tiles, tok, feat = queries.shape
    heads = window_time.shape[0]
    dim = feat // heads
    blocks = lax.axis_size("seq")
    per_source = (heads + blocks - 2) // (blocks - 1)
    chunks = heads // CHUNK_HEADS
    send_meta, recv_meta, biases = listed(
        block_list, list_len, window_time, window_rows, blocks, heads, per_source
    )
    kind = keys.dtype
    smem = pl.BlockSpec(memory_space=pltpu.SMEM)
    vmem = pl.BlockSpec(memory_space=pltpu.VMEM)
    anywhere = pl.BlockSpec(memory_space=pl.ANY)
    dma = pltpu.SemaphoreType.DMA
    return pl.pallas_call(
        functools.partial(kernel, blocks, heads, tok, dim, per_source),
        out_shape=jax.ShapeDtypeStruct(queries.shape, queries.dtype),
        in_specs=[smem, smem, smem, anywhere, anywhere, anywhere],
        out_specs=vmem,
        scratch_shapes=[
            pltpu.VMEM((heads, tiles, tok, dim), kind),
            pltpu.VMEM((2, heads, tiles, tok, dim), kind),
            pltpu.VMEM((2, heads, tok, dim), kind),
            pltpu.VMEM((2, heads, tiles, tok, dim), kind),
            pltpu.VMEM((2, heads, tok, dim), kind),
            pltpu.VMEM((2, heads, tiles, tok, dim), kind),
            pltpu.VMEM((2, heads, tok, dim), kind),
            pltpu.VMEM((blocks, per_source * LIST, 2, tok, dim), kind),
            pltpu.VMEM((blocks, per_source * LIST, 2, tok, dim), kind),
            pltpu.VMEM((heads, tiles, tok, dim), jnp.float32),
            pltpu.VMEM((heads, tiles, tok, 1), jnp.float32),
            pltpu.VMEM((heads, tiles, tok, 1), jnp.float32),
            dma((3, heads)),
            dma((2,)),
            dma((chunks, 2)),
            dma((chunks, 2)),
            dma((chunks, 2)),
            dma((chunks, 2)),
            dma((blocks, 2)),
        ],
        compiler_params=pltpu.CompilerParams(
            collective_id=0, has_side_effects=True, vmem_limit_bytes=56 * 1024 * 1024
        ),
        cost_estimate=pl.CostEstimate(
            flops=4 * heads * tiles * 10 * tok * tok * dim,
            bytes_accessed=4 * tiles * tok * feat * 2,
            transcendentals=heads * tiles * 10 * tok * tok,
        ),
    )(send_meta, recv_meta, biases, queries, keys, values)


def solution(mesh):
    return jax.shard_map(
        on_device,
        mesh=mesh,
        in_specs=(
            P(("group", "seq"), None, None),
            P(("group", "seq"), None, None),
            P(("group", "seq"), None, None),
            P("group", None, None),
            P("group", None),
            P(),
            P(),
        ),
        out_specs=P(("group", "seq"), None, None),
        check_vma=False,
    )
```

```python
import functools
import math

import jax
import jax.numpy as jnp
from jax import lax
from jax.experimental import pallas as pl
from jax.experimental.pallas import tpu as pltpu
from jax.sharding import PartitionSpec as P

ROW_TILES = 3
ROW_BLOCKS = 2
LIST = 2
REACH_STEPS = (8, 10, 12, 14)
BIG_NEG = -1e30


def kernel(
    blocks, heads, tok, dim, per_source, chunk_heads, chunks, detours,
    send_meta, recv_meta, order, biases, q_hbm, k_hbm, v_hbm, out_ref,
    qs, kv, packed, edge, passing, near, near_edge, relayed, relayed_edge, far_out, far_in, acc, top, total,
    load_sem, edge_sem, pass_sem, near_sem, near_edge_sem, relay_sem, relay_edge_sem, far_sem,
):
    me = lax.axis_index("seq")
    side = lax.rem(me, ROW_BLOCKS)
    time = me // ROW_BLOCKS
    times = blocks // ROW_BLOCKS
    odd = lax.rem(time, 2)
    partner = me + 1 - 2 * side
    mirror = me + ROW_BLOCKS * (1 - 2 * odd)
    ahead = 2 * (1 - 2 * odd)
    gives = jnp.logical_and(time + ahead >= 0, time + ahead < times)
    takes = jnp.logical_and(time - ahead >= 0, time - ahead < times)
    relay_to = me + ROW_BLOCKS * ahead
    edge_tile = 2 - 2 * side
    other_tile = 2 * side
    direct = chunks - detours

    def remote(src, dst, sems, device):
        return pltpu.make_async_remote_copy(
            src_ref=src, dst_ref=dst, send_sem=sems.at[0], recv_sem=sems.at[1],
            device_id={"seq": device}, device_id_type=pl.DeviceIdType.MESH,
        )

    def part_of(chunk):
        return pl.ds(chunk * chunk_heads, chunk_heads)

    def near_copy(chunk):
        part = part_of(chunk)
        return remote(packed.at[:, part], near.at[:, part], near_sem.at[chunk], mirror)

    def near_edge_copy(chunk):
        part = part_of(chunk)
        return remote(
            near.at[:, part, edge_tile], near_edge.at[:, part],
            near_edge_sem.at[chunk], partner,
        )

    def pass_copy(chunk):
        return remote(
            packed.at[:, part_of(direct + chunk)], passing.at[:, part_of(chunk)],
            pass_sem.at[chunk], me - ROW_BLOCKS * ahead,
        )

    def pass_on_copy(chunk):
        return remote(
            passing.at[:, part_of(chunk)], relayed.at[:, part_of(direct + chunk)],
            relay_sem.at[direct + chunk], mirror,
        )

    def relay_copy(chunk):
        part = part_of(chunk)
        return remote(
            near.at[:, part], relayed.at[:, part], relay_sem.at[chunk], relay_to
        )

    def relay_edge_copy(chunk):
        part = part_of(chunk)
        return remote(
            relayed.at[:, part, edge_tile], relayed_edge.at[:, part],
            relay_edge_sem.at[chunk], partner,
        )

    def far_copy(offset):
        return remote(
            far_out.at[offset], far_in.at[offset], far_sem.at[offset], lax.rem(me + offset, blocks)
        )

    def loads(head):
        cols = pl.ds(pl.multiple_of(head * dim, dim), dim)
        return [
            pltpu.make_async_copy(array.at[:, :, cols], held, load_sem.at[which, head])
            for which, (array, held) in enumerate(
                ((k_hbm, kv.at[0, head]), (v_hbm, kv.at[1, head]), (q_hbm, qs.at[head]))
            )
        ]

    def start_loads(head, carry):
        for copy in loads(head):
            copy.start()
        return carry

    def end_loads(head, carry):
        for copy in loads(head):
            copy.wait()
        return carry

    lax.fori_loop(0, heads, start_loads, 0)
    barrier = pltpu.get_barrier_semaphore()

    def greet(offset, carry):
        pl.semaphore_signal(
            barrier, inc=1, device_id={"seq": lax.rem(me + offset, blocks)},
            device_id_type=pl.DeviceIdType.MESH,
        )
        return carry

    lax.fori_loop(1, blocks, greet, 0)
    lax.fori_loop(0, heads, end_loads, 0)
    pl.semaphore_wait(barrier, blocks - 1)

    edge_copy = remote(kv.at[:, :, edge_tile], edge, edge_sem, partner)
    edge_copy.start()

    def start_near(chunk, carry):
        near_copy(chunk).start()
        return carry

    def pack(index, carry):
        head = order[0, index]
        for part in range(2):
            for tile in range(ROW_TILES):
                packed[part, index, tile] = kv[part, head, tile]
        return carry

    lax.fori_loop(0, chunks * chunk_heads, pack, 0)

    @pl.when(takes)
    def _():
        for chunk in range(detours):
            pass_copy(chunk).start()

    lax.fori_loop(0, chunks, start_near, 0)

    def start_far(offset, carry):
        target = lax.rem(me + offset, blocks)
        for pair in range(per_source):
            head = send_meta[target, 3 * pair]
            for which in range(LIST):
                tile = send_meta[target, 3 * pair + 1 + which]
                for part in range(2):
                    far_out[offset, pair * LIST + which, part] = kv[part, head, tile]
        far_copy(offset).start()
        return carry

    lax.fori_loop(1, blocks, start_far, 0)

    factor = math.log2(math.e) / math.sqrt(dim)

    def scores_of(query, key, bias):
        product = lax.dot_general(
            query, key, (((1,), (1,)), ((), ())), preferred_element_type=jnp.float32
        )
        return product * factor + bias

    def fold(head, tile, scores, value, first):
        high = jnp.max(scores, axis=1, keepdims=True)
        if not first:
            old = top[head, tile]
            high = jnp.maximum(high, old)
            shrink = jnp.exp2(old - high)
        weights = jnp.exp2(scores - high)
        amount = jnp.sum(weights, axis=1, keepdims=True)
        mixed = jnp.dot(
            weights.astype(jnp.bfloat16), value, preferred_element_type=jnp.float32
        )
        if not first:
            amount = amount + total[head, tile] * shrink
            mixed = mixed + acc[head, tile] * shrink
        return high, amount, mixed

    def keep(head, tile, state):
        top[head, tile], total[head, tile], acc[head, tile] = state

    def window_row(index, rows, edges, own):
        head = order[0, index]
        spot = head if own else index
        along = jnp.float32(0.0) if own else biases[0, head]
        lane = lax.broadcasted_iota(jnp.int32, (1, 3 * tok), 1)
        bias = jnp.where(lane < tok, along, biases[1 if own else 2, head])
        k_mid, v_mid = rows[0, spot, 1], rows[1, spot, 1]
        k_edge, v_edge = rows[0, spot, edge_tile], rows[1, spot, edge_tile]
        k_other, v_other = rows[0, spot, other_tile], rows[1, spot, other_tile]
        k_out, v_out = edges[0, spot], edges[1, spot]
        for tile, key, value in (
            (1, (k_mid, k_edge, k_other), (v_mid, v_edge, v_other)),
            (edge_tile, (k_edge, k_mid, k_out), (v_edge, v_mid, v_out)),
            (other_tile, (k_other, k_mid), (v_other, v_mid)),
        ):
            key = jnp.concatenate(key, axis=0)
            value = jnp.concatenate(value, axis=0)
            scores = scores_of(qs[head, tile], key, bias[:, : key.shape[0]])
            keep(index, tile, fold(index, tile, scores, value, own))

    edge_copy.wait_recv()

    def own_row(head, carry):
        window_row(head, kv, edge, True)
        return carry

    lax.fori_loop(0, heads, own_row, 0)

    def near_rows(chunk):
        def step(inner, carry):
            window_row(chunk * chunk_heads + inner, near, near_edge, False)
            return carry

        lax.fori_loop(0, chunk_heads, step, 0)

    def relayed_rows(chunk):
        def step(inner, carry):
            window_row(chunk * chunk_heads + inner, relayed, relayed_edge, False)
            return carry

        lax.fori_loop(0, chunk_heads, step, 0)

    def relay_arrived(chunk):
        relay_copy(chunk).wait_recv()
        relay_edge_copy(chunk).start()

    def relay_used(chunk):
        relay_edge_copy(chunk).wait_recv()
        relayed_rows(chunk)

    def time_chunk(chunk, carry):
        near_copy(chunk).wait_recv()
        near_edge_copy(chunk).start()

        @pl.when(jnp.logical_and(gives, chunk < direct))
        def _():
            relay_copy(chunk).start()

        @pl.when(jnp.logical_and(gives, jnp.logical_and(chunk > 0, chunk <= detours)))
        def _():
            pass_copy(chunk - 1).wait_recv()
            pass_on_copy(chunk - 1).start()

        @pl.when(jnp.logical_and(takes, chunk > 0))
        def _():
            relay_arrived(chunk - 1)

        near_edge_copy(chunk).wait_recv()
        near_rows(chunk)

        @pl.when(jnp.logical_and(takes, chunk > 0))
        def _():
            relay_used(chunk - 1)

        return carry

    lax.fori_loop(0, chunks, time_chunk, 0)

    @pl.when(takes)
    def _():
        relay_arrived(chunks - 1)
        relay_used(chunks - 1)

    def far_arrived(offset, carry):
        far_copy(offset).wait_recv()
        return carry

    lax.fori_loop(1, blocks, far_arrived, 0)

    def far_head(head, carry):
        cols = pl.ds(pl.multiple_of(head * dim, dim), dim)
        offset, slot = recv_meta[0, head], recv_meta[1, head]
        key = jnp.concatenate([far_in[offset, slot + w, 0] for w in range(LIST)], axis=0)
        value = jnp.concatenate([far_in[offset, slot + w, 1] for w in range(LIST)], axis=0)
        lane = lax.broadcasted_iota(jnp.int32, (1, LIST * tok), 1)
        for tile in range(ROW_TILES):
            bias = jnp.where(lane < tok, biases[3 + 2 * tile, head], biases[4 + 2 * tile, head])
            scores = scores_of(qs[head, tile], key, bias)
            _, amount, mixed = fold(order[1, head], tile, scores, value, False)
            out_ref[tile, :, cols] = (mixed / amount).astype(out_ref.dtype)
        return carry

    lax.fori_loop(0, heads, far_head, 0)

    edge_copy.wait_send()

    def sent(chunk, carry):
        near_copy(chunk).wait_send()
        near_edge_copy(chunk).wait_send()

        @pl.when(jnp.logical_and(gives, chunk < direct))
        def _():
            relay_copy(chunk).wait_send()

        @pl.when(jnp.logical_and(gives, chunk < detours))
        def _():
            pass_on_copy(chunk).wait_send()

        @pl.when(jnp.logical_and(takes, chunk < detours))
        def _():
            pass_copy(chunk).wait_send()

        @pl.when(takes)
        def _():
            relay_edge_copy(chunk).wait_send()

        return carry

    lax.fori_loop(0, chunks, sent, 0)

    def far_sent(offset, carry):
        far_copy(offset).wait_send()
        return carry

    lax.fori_loop(1, blocks, far_sent, 0)


def listed(block_list, list_len, window_time, window_rows, blocks, heads, per_source):
    me = lax.axis_index("seq")
    lists = block_list.reshape(blocks, ROW_TILES, heads, LIST)
    lens = list_len.reshape(blocks, ROW_TILES, heads, 1)
    live = jnp.arange(LIST, dtype=jnp.int32) < lens
    low = jnp.min(jnp.where(live, lists, jnp.int32(1 << 20)), axis=(1, 3))
    high = jnp.max(jnp.where(live, lists, jnp.int32(-1)), axis=(1, 3))
    source = low // ROW_TILES
    low_tile, high_tile = low % ROW_TILES, high % ROW_TILES
    number = jnp.arange(heads, dtype=jnp.int32)[None, :]
    mine = source == me
    first = jnp.min(jnp.where(mine, number, heads), axis=1, keepdims=True)
    first = jnp.where(first == heads, 0, first)
    last = jnp.max(jnp.where(mine, number, 0), axis=1, keepdims=True)
    columns = []
    for pick in (first, last)[:per_source]:
        hit = number == pick
        columns += [
            pick[:, 0],
            jnp.sum(jnp.where(hit, low_tile, 0), axis=1),
            jnp.sum(jnp.where(hit, high_tile, 0), axis=1),
        ]
    send_meta = jnp.stack(columns, axis=1)

    def own(table):
        return lax.dynamic_index_in_dim(table, me, 0, keepdims=False)

    own_source, own_low, own_high = own(source), own(low), own(high)
    own_lists, own_live = own(lists), own(live)
    earlier = (own_source[None, :] == own_source[:, None]) & (number < number.T)
    rank = jnp.minimum(jnp.any(earlier, axis=1).astype(jnp.int32), per_source - 1)
    recv_meta = jnp.stack([(me - own_source + blocks) % blocks, LIST * rank], axis=0)
    in_time, in_rows = window_time > 0, window_rows > 0
    rows = [in_time, in_rows, in_time & in_rows]
    for tile in range(ROW_TILES):
        for wanted in (own_low, own_high):
            found = own_live[tile] & (own_lists[tile] == wanted[:, None])
            rows.append(jnp.any(found, axis=1))
    biases = jnp.where(jnp.stack(rows, axis=0), 0.0, BIG_NEG).astype(jnp.float32)
    rank = jnp.sum(
        (window_time[None, :] > window_time[:, None])
        | ((window_time[None, :] == window_time[:, None]) & (number < number.T)),
        axis=1,
        dtype=jnp.int32,
    )
    head_at = jnp.sum(jnp.where(rank[None, :] == number.T, number, 0), axis=1)
    return send_meta, recv_meta, jnp.stack([head_at, rank], axis=0), biases


def on_device(queries, keys, values, block_list, list_len, window_time, window_rows):
    tiles, tok, feat = queries.shape
    heads = window_time.shape[0]
    dim = feat // heads
    blocks = lax.axis_size("seq")
    per_source = (heads + blocks - 2) // (blocks - 1)
    meta = listed(
        block_list, list_len, window_time, window_rows, blocks, heads, per_source
    )
    steps = [count for count in REACH_STEPS if count < heads] + [heads]
    reaching = jnp.sum((window_time > 0).astype(jnp.int32))
    branch = sum((reaching > count).astype(jnp.int32) for count in steps[:-1])
    calls = [
        functools.partial(attend, count, number, blocks, heads, per_source)
        for number, count in enumerate(steps)
    ]
    return lax.switch(branch, calls, *meta, queries, keys, values)


def attend(reaching, number, blocks, heads, per_source, *operands):
    queries, keys = operands[-3:-1]
    tiles, tok, feat = queries.shape
    dim = feat // heads
    chunk_heads = 4 if reaching == 20 else 2
    chunks = reaching // chunk_heads
    detours = 2 * chunks // 5
    kind = keys.dtype
    smem = pl.BlockSpec(memory_space=pltpu.SMEM)
    vmem = pl.BlockSpec(memory_space=pltpu.VMEM)
    anywhere = pl.BlockSpec(memory_space=pl.ANY)
    dma = pltpu.SemaphoreType.DMA
    return pl.pallas_call(
        functools.partial(
            kernel, blocks, heads, tok, dim, per_source, chunk_heads, chunks, detours
        ),
        out_shape=jax.ShapeDtypeStruct(queries.shape, queries.dtype),
        in_specs=[smem] * 4 + [anywhere] * 3,
        out_specs=vmem,
        scratch_shapes=[
            pltpu.VMEM((heads, tiles, tok, dim), kind),
            pltpu.VMEM((2, heads, tiles, tok, dim), kind),
            pltpu.VMEM((2, reaching, tiles, tok, dim), kind),
            pltpu.VMEM((2, heads, tok, dim), kind),
            pltpu.VMEM((2, detours * chunk_heads, tiles, tok, dim), kind),
            pltpu.VMEM((2, reaching, tiles, tok, dim), kind),
            pltpu.VMEM((2, reaching, tok, dim), kind),
            pltpu.VMEM((2, reaching, tiles, tok, dim), kind),
            pltpu.VMEM((2, reaching, tok, dim), kind),
            pltpu.VMEM((blocks, per_source * LIST, 2, tok, dim), kind),
            pltpu.VMEM((blocks, per_source * LIST, 2, tok, dim), kind),
            pltpu.VMEM((heads, tiles, tok, dim), jnp.float32),
            pltpu.VMEM((heads, tiles, tok, 1), jnp.float32),
            pltpu.VMEM((heads, tiles, tok, 1), jnp.float32),
            dma((3, heads)),
            dma((2,)),
            dma((detours, 2)),
            dma((chunks, 2)),
            dma((chunks, 2)),
            dma((chunks, 2)),
            dma((chunks, 2)),
            dma((blocks, 2)),
        ],
        compiler_params=pltpu.CompilerParams(
            collective_id=number, has_side_effects=True, vmem_limit_bytes=56 * 1024 * 1024
        ),
        cost_estimate=pl.CostEstimate(
            flops=4 * heads * tiles * 10 * tok * tok * dim,
            bytes_accessed=4 * tiles * tok * feat * 2,
            transcendentals=heads * tiles * 10 * tok * tok,
        ),
    )(*operands)


def solution(mesh):
    return jax.shard_map(
        on_device,
        mesh=mesh,
        in_specs=(
            P(("group", "seq"), None, None),
            P(("group", "seq"), None, None),
            P(("group", "seq"), None, None),
            P("group", None, None),
            P("group", None),
            P(),
            P(),
        ),
        out_specs=P(("group", "seq"), None, None),
        check_vma=False,
    )
```

```python
import functools
import math

import jax
import jax.numpy as jnp
from jax import lax
from jax.experimental import pallas as pl
from jax.experimental.pallas import tpu as pltpu
from jax.sharding import PartitionSpec as P

ROW_TILES = 3
ROW_BLOCKS = 2
LIST = 2
REACH_STEPS = (8, 10, 12, 14)
BIG_NEG = -1e30


def kernel(
    blocks, heads, tok, dim, per_source, chunk_heads, chunks, detours,
    send_meta, recv_meta, order, biases, q_hbm, k_hbm, v_hbm, out_ref,
    qs, kv, packed, edge, passing, near, near_edge, relayed, relayed_edge, far_out, far_in, acc, top, total,
    load_sem, edge_sem, pass_sem, near_sem, near_edge_sem, relay_sem, relay_edge_sem, far_sem,
):
    me = lax.axis_index("seq")
    side = lax.rem(me, ROW_BLOCKS)
    time = me // ROW_BLOCKS
    times = blocks // ROW_BLOCKS
    odd = lax.rem(time, 2)
    partner = me + 1 - 2 * side
    mirror = me + ROW_BLOCKS * (1 - 2 * odd)
    ahead = 2 * (1 - 2 * odd)
    gives = jnp.logical_and(time + ahead >= 0, time + ahead < times)
    takes = jnp.logical_and(time - ahead >= 0, time - ahead < times)
    relay_to = me + ROW_BLOCKS * ahead
    edge_tile = 2 - 2 * side
    other_tile = 2 * side
    direct = chunks - detours

    def remote(src, dst, sems, device):
        return pltpu.make_async_remote_copy(
            src_ref=src, dst_ref=dst, send_sem=sems.at[0], recv_sem=sems.at[1],
            device_id={"seq": device}, device_id_type=pl.DeviceIdType.MESH,
        )

    def part_of(chunk):
        return pl.ds(chunk * chunk_heads, chunk_heads)

    def near_copy(chunk):
        part = part_of(chunk)
        return remote(packed.at[:, part], near.at[:, part], near_sem.at[chunk], mirror)

    def near_edge_copy(chunk):
        part = part_of(chunk)
        return remote(
            near.at[:, part, edge_tile], near_edge.at[:, part],
            near_edge_sem.at[chunk], partner,
        )

    def pass_copy(chunk):
        return remote(
            packed.at[:, part_of(direct + chunk)], passing.at[:, part_of(chunk)],
            pass_sem.at[chunk], me - ROW_BLOCKS * ahead,
        )

    def pass_on_copy(chunk):
        return remote(
            passing.at[:, part_of(chunk)], relayed.at[:, part_of(direct + chunk)],
            relay_sem.at[direct + chunk], mirror,
        )

    def relay_copy(chunk):
        part = part_of(chunk)
        return remote(
            near.at[:, part], relayed.at[:, part], relay_sem.at[chunk], relay_to
        )

    def relay_edge_copy(chunk):
        part = part_of(chunk)
        return remote(
            relayed.at[:, part, edge_tile], relayed_edge.at[:, part],
            relay_edge_sem.at[chunk], partner,
        )

    def far_target(offset):
        plane = lax.rem(me // 4 + offset // 4, blocks // 4)
        return 4 * plane + 2 * lax.rem(odd + offset // 2, 2) + lax.rem(side + offset, 2)

    def far_copy(offset):
        return remote(
            far_out.at[offset], far_in.at[offset], far_sem.at[offset], far_target(offset)
        )

    def loads(head):
        cols = pl.ds(pl.multiple_of(head * dim, dim), dim)
        return [
            pltpu.make_async_copy(array.at[:, :, cols], held, load_sem.at[which, head])
            for which, (array, held) in enumerate(
                ((k_hbm, kv.at[0, head]), (v_hbm, kv.at[1, head]), (q_hbm, qs.at[head]))
            )
        ]

    def start_loads(head, carry):
        for copy in loads(head):
            copy.start()
        return carry

    def end_loads(head, carry):
        for copy in loads(head):
            copy.wait()
        return carry

    lax.fori_loop(0, heads, start_loads, 0)
    barrier = pltpu.get_barrier_semaphore()

    def greet(offset, carry):
        pl.semaphore_signal(
            barrier, inc=1, device_id={"seq": lax.rem(me + offset, blocks)},
            device_id_type=pl.DeviceIdType.MESH,
        )
        return carry

    lax.fori_loop(1, blocks, greet, 0)
    lax.fori_loop(0, heads, end_loads, 0)
    pl.semaphore_wait(barrier, blocks - 1)

    edge_copy = remote(kv.at[:, :, edge_tile], edge, edge_sem, partner)
    edge_copy.start()

    def start_near(chunk, carry):
        near_copy(chunk).start()
        return carry

    def pack(index, carry):
        head = order[0, index]
        for part in range(2):
            for tile in range(ROW_TILES):
                packed[part, index, tile] = kv[part, head, tile]
        return carry

    lax.fori_loop(0, chunks * chunk_heads, pack, 0)

    @pl.when(takes)
    def _():
        for chunk in range(detours):
            pass_copy(chunk).start()

    lax.fori_loop(0, chunks, start_near, 0)

    def send_far(offset):
        target = far_target(offset)
        for pair in range(per_source):
            head = send_meta[target, 3 * pair]
            for which in range(LIST):
                tile = send_meta[target, 3 * pair + 1 + which]
                for part in range(2):
                    far_out[offset, pair * LIST + which, part] = kv[part, head, tile]
        far_copy(offset).start()

    def far_straight(place, carry):
        plane = lax.rem(place // 2 + blocks // 8, blocks // 4)
        offset = 4 * plane + lax.rem(place, 2)

        @pl.when(offset > 0)
        def _():
            send_far(offset)

        return carry

    def far_across(place, carry):
        plane = lax.rem(place // 2 + blocks // 8, blocks // 4)
        send_far(4 * plane + 2 + lax.rem(place, 2))
        return carry

    lax.fori_loop(0, blocks // 2, far_straight, 0)

    factor = math.log2(math.e) / math.sqrt(dim)

    def scores_of(query, key, bias):
        product = lax.dot_general(
            query, key, (((1,), (1,)), ((), ())), preferred_element_type=jnp.float32
        )
        return product * factor + bias

    def fold(head, tile, scores, value, first):
        high = jnp.max(scores, axis=1, keepdims=True)
        if not first:
            old = top[head, tile]
            high = jnp.maximum(high, old)
            shrink = jnp.exp2(old - high)
        weights = jnp.exp2(scores - high)
        amount = jnp.sum(weights, axis=1, keepdims=True)
        mixed = jnp.dot(
            weights.astype(jnp.bfloat16), value, preferred_element_type=jnp.float32
        )
        if not first:
            amount = amount + total[head, tile] * shrink
            mixed = mixed + acc[head, tile] * shrink
        return high, amount, mixed

    def keep(head, tile, state):
        top[head, tile], total[head, tile], acc[head, tile] = state

    def window_row(index, rows, edges, own):
        head = order[0, index]
        spot = head if own else index
        along = jnp.float32(0.0) if own else biases[0, head]
        lane = lax.broadcasted_iota(jnp.int32, (1, 3 * tok), 1)
        bias = jnp.where(lane < tok, along, biases[1 if own else 2, head])
        k_mid, v_mid = rows[0, spot, 1], rows[1, spot, 1]
        k_edge, v_edge = rows[0, spot, edge_tile], rows[1, spot, edge_tile]
        k_other, v_other = rows[0, spot, other_tile], rows[1, spot, other_tile]
        k_out, v_out = edges[0, spot], edges[1, spot]
        for tile, key, value in (
            (1, (k_mid, k_edge, k_other), (v_mid, v_edge, v_other)),
            (edge_tile, (k_edge, k_mid, k_out), (v_edge, v_mid, v_out)),
            (other_tile, (k_other, k_mid), (v_other, v_mid)),
        ):
            key = jnp.concatenate(key, axis=0)
            value = jnp.concatenate(value, axis=0)
            scores = scores_of(qs[head, tile], key, bias[:, : key.shape[0]])
            keep(index, tile, fold(index, tile, scores, value, own))

    edge_copy.wait_recv()

    def own_row(head, carry):
        window_row(head, kv, edge, True)
        return carry

    lax.fori_loop(0, heads, own_row, 0)

    def near_rows(chunk):
        def step(inner, carry):
            window_row(chunk * chunk_heads + inner, near, near_edge, False)
            return carry

        lax.fori_loop(0, chunk_heads, step, 0)

    def relayed_rows(chunk):
        def step(inner, carry):
            window_row(chunk * chunk_heads + inner, relayed, relayed_edge, False)
            return carry

        lax.fori_loop(0, chunk_heads, step, 0)

    def relay_arrived(chunk):
        relay_copy(chunk).wait_recv()
        relay_edge_copy(chunk).start()

    def relay_used(chunk):
        relay_edge_copy(chunk).wait_recv()
        relayed_rows(chunk)

    def time_chunk(chunk, carry):
        near_copy(chunk).wait_recv()
        near_edge_copy(chunk).start()

        @pl.when(jnp.logical_and(gives, chunk < direct))
        def _():
            relay_copy(chunk).start()

        @pl.when(jnp.logical_and(gives, jnp.logical_and(chunk > 0, chunk <= detours)))
        def _():
            pass_copy(chunk - 1).wait_recv()
            pass_on_copy(chunk - 1).start()

        lax.fori_loop(
            chunk * (blocks // 2) // chunks, (chunk + 1) * (blocks // 2) // chunks, far_across, 0
        )
        near_edge_copy(chunk).wait_recv()
        near_rows(chunk)
        return carry

    lax.fori_loop(0, chunks, time_chunk, 0)

    def relayed_chunk(chunk, carry):
        relay_arrived(chunk)

        @pl.when(chunk > 0)
        def _():
            relay_used(chunk - 1)

        return carry

    @pl.when(takes)
    def _():
        lax.fori_loop(0, chunks, relayed_chunk, 0)
        relay_used(chunks - 1)

    def far_arrived(offset, carry):
        far_copy(offset).wait_recv()
        return carry

    lax.fori_loop(1, blocks, far_arrived, 0)

    def far_head(head, carry):
        cols = pl.ds(pl.multiple_of(head * dim, dim), dim)
        offset, slot = recv_meta[0, head], recv_meta[1, head]
        key = jnp.concatenate([far_in[offset, slot + w, 0] for w in range(LIST)], axis=0)
        value = jnp.concatenate([far_in[offset, slot + w, 1] for w in range(LIST)], axis=0)
        lane = lax.broadcasted_iota(jnp.int32, (1, LIST * tok), 1)
        for tile in range(ROW_TILES):
            bias = jnp.where(lane < tok, biases[3 + 2 * tile, head], biases[4 + 2 * tile, head])
            scores = scores_of(qs[head, tile], key, bias)
            _, amount, mixed = fold(order[1, head], tile, scores, value, False)
            out_ref[tile, :, cols] = (mixed / amount).astype(out_ref.dtype)
        return carry

    lax.fori_loop(0, heads, far_head, 0)

    edge_copy.wait_send()

    def sent(chunk, carry):
        near_copy(chunk).wait_send()
        near_edge_copy(chunk).wait_send()

        @pl.when(jnp.logical_and(gives, chunk < direct))
        def _():
            relay_copy(chunk).wait_send()

        @pl.when(jnp.logical_and(gives, chunk < detours))
        def _():
            pass_on_copy(chunk).wait_send()

        @pl.when(jnp.logical_and(takes, chunk < detours))
        def _():
            pass_copy(chunk).wait_send()

        @pl.when(takes)
        def _():
            relay_edge_copy(chunk).wait_send()

        return carry

    lax.fori_loop(0, chunks, sent, 0)

    def far_sent(offset, carry):
        far_copy(offset).wait_send()
        return carry

    lax.fori_loop(1, blocks, far_sent, 0)


def listed(block_list, list_len, window_time, window_rows, blocks, heads, per_source):
    me = lax.axis_index("seq")
    lists = block_list.reshape(blocks, ROW_TILES, heads, LIST)
    lens = list_len.reshape(blocks, ROW_TILES, heads, 1)
    live = jnp.arange(LIST, dtype=jnp.int32) < lens
    low = jnp.min(jnp.where(live, lists, jnp.int32(1 << 20)), axis=(1, 3))
    high = jnp.max(jnp.where(live, lists, jnp.int32(-1)), axis=(1, 3))
    source = low // ROW_TILES
    low_tile, high_tile = low % ROW_TILES, high % ROW_TILES
    number = jnp.arange(heads, dtype=jnp.int32)[None, :]
    mine = source == me
    first = jnp.min(jnp.where(mine, number, heads), axis=1, keepdims=True)
    first = jnp.where(first == heads, 0, first)
    last = jnp.max(jnp.where(mine, number, 0), axis=1, keepdims=True)
    columns = []
    for pick in (first, last)[:per_source]:
        hit = number == pick
        columns += [
            pick[:, 0],
            jnp.sum(jnp.where(hit, low_tile, 0), axis=1),
            jnp.sum(jnp.where(hit, high_tile, 0), axis=1),
        ]
    send_meta = jnp.stack(columns, axis=1)

    def own(table):
        return lax.dynamic_index_in_dim(table, me, 0, keepdims=False)

    own_source, own_low, own_high = own(source), own(low), own(high)
    own_lists, own_live = own(lists), own(live)
    earlier = (own_source[None, :] == own_source[:, None]) & (number < number.T)
    rank = jnp.minimum(jnp.any(earlier, axis=1).astype(jnp.int32), per_source - 1)
    offset = (
        4 * ((me // 4 - own_source // 4 + blocks // 4) % (blocks // 4))
        + 2 * ((me // 2 + own_source // 2) % 2)
        + (me + own_source) % 2
    )
    recv_meta = jnp.stack([offset, LIST * rank], axis=0)
    in_time, in_rows = window_time > 0, window_rows > 0
    rows = [in_time, in_rows, in_time & in_rows]
    for tile in range(ROW_TILES):
        for wanted in (own_low, own_high):
            found = own_live[tile] & (own_lists[tile] == wanted[:, None])
            rows.append(jnp.any(found, axis=1))
    biases = jnp.where(jnp.stack(rows, axis=0), 0.0, BIG_NEG).astype(jnp.float32)
    rank = jnp.sum(
        (window_time[None, :] > window_time[:, None])
        | ((window_time[None, :] == window_time[:, None]) & (number < number.T)),
        axis=1,
        dtype=jnp.int32,
    )
    head_at = jnp.sum(jnp.where(rank[None, :] == number.T, number, 0), axis=1)
    return send_meta, recv_meta, jnp.stack([head_at, rank], axis=0), biases


def on_device(queries, keys, values, block_list, list_len, window_time, window_rows):
    tiles, tok, feat = queries.shape
    heads = window_time.shape[0]
    dim = feat // heads
    blocks = lax.axis_size("seq")
    per_source = (heads + blocks - 2) // (blocks - 1)
    meta = listed(
        block_list, list_len, window_time, window_rows, blocks, heads, per_source
    )
    steps = [count for count in REACH_STEPS if count < heads] + [heads]
    reaching = jnp.sum((window_time > 0).astype(jnp.int32))
    branch = sum((reaching > count).astype(jnp.int32) for count in steps[:-1])
    calls = [
        functools.partial(attend, count, number, blocks, heads, per_source)
        for number, count in enumerate(steps)
    ]
    return lax.switch(branch, calls, *meta, queries, keys, values)


def attend(reaching, number, blocks, heads, per_source, *operands):
    queries, keys = operands[-3:-1]
    tiles, tok, feat = queries.shape
    dim = feat // heads
    chunk_heads = 4 if reaching == 20 else 2
    chunks = reaching // chunk_heads
    detours = 2 * chunks // 5
    kind = keys.dtype
    smem = pl.BlockSpec(memory_space=pltpu.SMEM)
    vmem = pl.BlockSpec(memory_space=pltpu.VMEM)
    anywhere = pl.BlockSpec(memory_space=pl.ANY)
    dma = pltpu.SemaphoreType.DMA
    return pl.pallas_call(
        functools.partial(
            kernel, blocks, heads, tok, dim, per_source, chunk_heads, chunks, detours
        ),
        out_shape=jax.ShapeDtypeStruct(queries.shape, queries.dtype),
        in_specs=[smem] * 4 + [anywhere] * 3,
        out_specs=vmem,
        scratch_shapes=[
            pltpu.VMEM((heads, tiles, tok, dim), kind),
            pltpu.VMEM((2, heads, tiles, tok, dim), kind),
            pltpu.VMEM((2, reaching, tiles, tok, dim), kind),
            pltpu.VMEM((2, heads, tok, dim), kind),
            pltpu.VMEM((2, detours * chunk_heads, tiles, tok, dim), kind),
            pltpu.VMEM((2, reaching, tiles, tok, dim), kind),
            pltpu.VMEM((2, reaching, tok, dim), kind),
            pltpu.VMEM((2, reaching, tiles, tok, dim), kind),
            pltpu.VMEM((2, reaching, tok, dim), kind),
            pltpu.VMEM((blocks, per_source * LIST, 2, tok, dim), kind),
            pltpu.VMEM((blocks, per_source * LIST, 2, tok, dim), kind),
            pltpu.VMEM((heads, tiles, tok, dim), jnp.float32),
            pltpu.VMEM((heads, tiles, tok, 1), jnp.float32),
            pltpu.VMEM((heads, tiles, tok, 1), jnp.float32),
            dma((3, heads)),
            dma((2,)),
            dma((detours, 2)),
            dma((chunks, 2)),
            dma((chunks, 2)),
            dma((chunks, 2)),
            dma((chunks, 2)),
            dma((blocks, 2)),
        ],
        compiler_params=pltpu.CompilerParams(
            collective_id=number, has_side_effects=True, vmem_limit_bytes=56 * 1024 * 1024
        ),
        cost_estimate=pl.CostEstimate(
            flops=4 * heads * tiles * 10 * tok * tok * dim,
            bytes_accessed=4 * tiles * tok * feat * 2,
            transcendentals=heads * tiles * 10 * tok * tok,
        ),
    )(*operands)


def solution(mesh):
    return jax.shard_map(
        on_device,
        mesh=mesh,
        in_specs=(
            P(("group", "seq"), None, None),
            P(("group", "seq"), None, None),
            P(("group", "seq"), None, None),
            P("group", None, None),
            P("group", None),
            P(),
            P(),
        ),
        out_specs=P(("group", "seq"), None, None),
        check_vma=False,
    )
```

```python
import functools
import math

import jax
import jax.numpy as jnp
from jax import lax
from jax.experimental import pallas as pl
from jax.experimental.pallas import tpu as pltpu
from jax.sharding import PartitionSpec as P

ROW_TILES = 3
ROW_BLOCKS = 2
LIST = 2
REACH_STEPS = (8, 10, 12, 14)
BIG_NEG = -1e30
ORDER_ROW = 6
HEAD_ROW = 8
LANES = 128


def kernel(
    blocks, heads, tok, dim, per_source, chunk_heads, chunks, detours,
    lists, lens, reach_time, reach_rows, q_hbm, k_hbm, v_hbm, out_ref,
    spread, table, meta, qs, kv, packed, edge, passing, near, near_edge, relayed, relayed_edge, far_out, far_in, acc, top, total,
    meta_sem, load_sem, edge_sem, pass_sem, near_sem, near_edge_sem, relay_sem, relay_edge_sem, far_sem,
):
    me = lax.axis_index("seq")
    side = lax.rem(me, ROW_BLOCKS)
    time = me // ROW_BLOCKS
    times = blocks // ROW_BLOCKS
    odd = lax.rem(time, 2)
    partner = me + 1 - 2 * side
    mirror = me + ROW_BLOCKS * (1 - 2 * odd)
    ahead = 2 * (1 - 2 * odd)
    gives = jnp.logical_and(time + ahead >= 0, time + ahead < times)
    takes = jnp.logical_and(time - ahead >= 0, time - ahead < times)
    relay_to = me + ROW_BLOCKS * ahead
    edge_tile = 2 - 2 * side
    other_tile = 2 * side
    direct = chunks - detours

    def remote(src, dst, sems, device):
        return pltpu.make_async_remote_copy(
            src_ref=src, dst_ref=dst, send_sem=sems.at[0], recv_sem=sems.at[1],
            device_id={"seq": device}, device_id_type=pl.DeviceIdType.MESH,
        )

    def part_of(chunk):
        return pl.ds(chunk * chunk_heads, chunk_heads)

    def near_copy(chunk):
        part = part_of(chunk)
        return remote(packed.at[:, part], near.at[:, part], near_sem.at[chunk], mirror)

    def near_edge_copy(chunk):
        part = part_of(chunk)
        return remote(
            near.at[:, part, edge_tile], near_edge.at[:, part],
            near_edge_sem.at[chunk], partner,
        )

    def pass_copy(chunk):
        return remote(
            packed.at[:, part_of(direct + chunk)], passing.at[:, part_of(chunk)],
            pass_sem.at[chunk], me - ROW_BLOCKS * ahead,
        )

    def pass_on_copy(chunk):
        return remote(
            passing.at[:, part_of(chunk)], relayed.at[:, part_of(direct + chunk)],
            relay_sem.at[direct + chunk], mirror,
        )

    def relay_copy(chunk):
        part = part_of(chunk)
        return remote(
            near.at[:, part], relayed.at[:, part], relay_sem.at[chunk], relay_to
        )

    def relay_edge_copy(chunk):
        part = part_of(chunk)
        return remote(
            relayed.at[:, part, edge_tile], relayed_edge.at[:, part],
            relay_edge_sem.at[chunk], partner,
        )

    def far_target(offset):
        plane = lax.rem(me // 4 + offset // 4, blocks // 4)
        return 4 * plane + 2 * lax.rem(odd + offset // 2, 2) + lax.rem(side + offset, 2)

    def far_copy(offset):
        return remote(
            far_out.at[offset], far_in.at[offset], far_sem.at[offset], far_target(offset)
        )

    def loads(head):
        cols = pl.ds(pl.multiple_of(head * dim, dim), dim)
        return [
            pltpu.make_async_copy(array.at[:, :, cols], held, load_sem.at[which, head])
            for which, (array, held) in enumerate(
                ((k_hbm, kv.at[0, head]), (v_hbm, kv.at[1, head]), (q_hbm, qs.at[head]))
            )
        ]

    def start_loads(head, carry):
        for copy in loads(head):
            copy.start()
        return carry

    def end_loads(head, carry):
        for copy in loads(head):
            copy.wait()
        return carry

    lax.fori_loop(0, heads, start_loads, 0)
    fill_table(
        lists, lens, reach_time, reach_rows, spread, table, me, blocks, heads, per_source
    )
    copy_meta = pltpu.make_async_copy(table, meta, meta_sem)
    copy_meta.start()
    barrier = pltpu.get_barrier_semaphore()

    def greet(offset, carry):
        pl.semaphore_signal(
            barrier, inc=1, device_id={"seq": lax.rem(me + offset, blocks)},
            device_id_type=pl.DeviceIdType.MESH,
        )
        return carry

    lax.fori_loop(1, blocks, greet, 0)
    lax.fori_loop(0, heads, end_loads, 0)
    pl.semaphore_wait(barrier, blocks - 1)
    copy_meta.wait()

    edge_copy = remote(kv.at[:, :, edge_tile], edge, edge_sem, partner)
    edge_copy.start()

    def start_near(chunk, carry):
        near_copy(chunk).start()
        return carry

    def pack(index, carry):
        head = meta[ORDER_ROW, index]
        for part in range(2):
            for tile in range(ROW_TILES):
                packed[part, index, tile] = kv[part, head, tile]
        return carry

    lax.fori_loop(0, chunks * chunk_heads, pack, 0)

    @pl.when(takes)
    def _():
        for chunk in range(detours):
            pass_copy(chunk).start()

    lax.fori_loop(0, chunks, start_near, 0)

    def send_far(offset):
        target = far_target(offset)
        for pair in range(per_source):
            head = meta[3 * pair, ROW_TILES * target]
            for which in range(LIST):
                tile = meta[3 * pair + 1 + which, ROW_TILES * target]
                for part in range(2):
                    far_out[offset, pair * LIST + which, part] = kv[part, head, tile]
        far_copy(offset).start()

    def far_straight(place, carry):
        plane = lax.rem(place // 2 + blocks // 8, blocks // 4)
        offset = 4 * plane + lax.rem(place, 2)

        @pl.when(offset > 0)
        def _():
            send_far(offset)

        return carry

    def far_across(place, carry):
        plane = lax.rem(place // 2 + blocks // 8, blocks // 4)
        send_far(4 * plane + 2 + lax.rem(place, 2))
        return carry

    lax.fori_loop(0, blocks // 2, far_straight, 0)

    factor = math.log2(math.e) / math.sqrt(dim)

    def scores_of(query, key, bias):
        product = lax.dot_general(
            query, key, (((1,), (1,)), ((), ())), preferred_element_type=jnp.float32
        )
        return product * factor + bias

    def fold(head, tile, scores, value, first):
        high = jnp.max(scores, axis=1, keepdims=True)
        if not first:
            old = top[head, tile]
            high = jnp.maximum(high, old)
            shrink = jnp.exp2(old - high)
        weights = jnp.exp2(scores - high)
        amount = jnp.sum(weights, axis=1, keepdims=True)
        mixed = jnp.dot(
            weights.astype(jnp.bfloat16), value, preferred_element_type=jnp.float32
        )
        if not first:
            amount = amount + total[head, tile] * shrink
            mixed = mixed + acc[head, tile] * shrink
        return high, amount, mixed

    def keep(head, tile, state):
        top[head, tile], total[head, tile], acc[head, tile] = state

    def closed(head, column):
        return (meta[HEAD_ROW + head, column].astype(jnp.float32) - 1.0) * -BIG_NEG

    def window_row(index, rows, edges, own):
        head = meta[ORDER_ROW, index]
        spot = head if own else index
        along = jnp.float32(0.0) if own else closed(head, 3)
        lane = lax.broadcasted_iota(jnp.int32, (1, 3 * tok), 1)
        bias = jnp.where(lane < tok, along, closed(head, 4 if own else 5))
        k_mid, v_mid = rows[0, spot, 1], rows[1, spot, 1]
        k_edge, v_edge = rows[0, spot, edge_tile], rows[1, spot, edge_tile]
        k_other, v_other = rows[0, spot, other_tile], rows[1, spot, other_tile]
        k_out, v_out = edges[0, spot], edges[1, spot]
        for tile, key, value in (
            (1, (k_mid, k_edge, k_other), (v_mid, v_edge, v_other)),
            (edge_tile, (k_edge, k_mid, k_out), (v_edge, v_mid, v_out)),
            (other_tile, (k_other, k_mid), (v_other, v_mid)),
        ):
            key = jnp.concatenate(key, axis=0)
            value = jnp.concatenate(value, axis=0)
            scores = scores_of(qs[head, tile], key, bias[:, : key.shape[0]])
            keep(index, tile, fold(index, tile, scores, value, own))

    def own_row(head, carry):
        window_row(head, kv, edge, True)
        return carry


    def near_rows(chunk):
        def step(inner, carry):
            window_row(chunk * chunk_heads + inner, near, near_edge, False)
            return carry

        lax.fori_loop(0, chunk_heads, step, 0)

    def relayed_rows(chunk):
        def step(inner, carry):
            window_row(chunk * chunk_heads + inner, relayed, relayed_edge, False)
            return carry

        lax.fori_loop(0, chunk_heads, step, 0)

    def relay_arrived(chunk):
        relay_copy(chunk).wait_recv()
        relay_edge_copy(chunk).start()

    def relay_used(chunk):
        relay_edge_copy(chunk).wait_recv()
        relayed_rows(chunk)

    def time_chunk(chunk, carry):
        near_copy(chunk).wait_recv()
        near_edge_copy(chunk).start()

        @pl.when(jnp.logical_and(gives, chunk < direct))
        def _():
            relay_copy(chunk).start()

        @pl.when(jnp.logical_and(gives, jnp.logical_and(chunk > 0, chunk <= detours)))
        def _():
            pass_copy(chunk - 1).wait_recv()
            pass_on_copy(chunk - 1).start()

        lax.fori_loop(
            chunk * (blocks // 2) // chunks, (chunk + 1) * (blocks // 2) // chunks, far_across, 0
        )
        @pl.when(chunk == 0)
        def _():
            edge_copy.wait_recv()

        lax.fori_loop(chunk * heads // chunks, (chunk + 1) * heads // chunks, own_row, 0)
        near_edge_copy(chunk).wait_recv()
        near_rows(chunk)
        return carry

    lax.fori_loop(0, chunks, time_chunk, 0)

    def relayed_chunk(chunk, carry):
        relay_arrived(chunk)

        @pl.when(chunk > 0)
        def _():
            relay_used(chunk - 1)

        return carry

    @pl.when(takes)
    def _():
        lax.fori_loop(0, chunks, relayed_chunk, 0)
        relay_used(chunks - 1)

    def far_arrived(offset, carry):
        far_copy(offset).wait_recv()
        return carry

    lax.fori_loop(1, blocks, far_arrived, 0)

    def far_head(head, carry):
        cols = pl.ds(pl.multiple_of(head * dim, dim), dim)
        offset, slot = meta[HEAD_ROW + head, 0], meta[HEAD_ROW + head, 1]
        key = jnp.concatenate([far_in[offset, slot + w, 0] for w in range(LIST)], axis=0)
        value = jnp.concatenate([far_in[offset, slot + w, 1] for w in range(LIST)], axis=0)
        lane = lax.broadcasted_iota(jnp.int32, (1, LIST * tok), 1)
        for tile in range(ROW_TILES):
            bias = jnp.where(
                lane < tok, closed(head, 6 + 2 * tile), closed(head, 7 + 2 * tile)
            )
            scores = scores_of(qs[head, tile], key, bias)
            _, amount, mixed = fold(meta[HEAD_ROW + head, 2], tile, scores, value, False)
            out_ref[tile, :, cols] = (mixed / amount).astype(out_ref.dtype)
        return carry

    lax.fori_loop(0, heads, far_head, 0, unroll=2)

    edge_copy.wait_send()

    def sent(chunk, carry):
        near_copy(chunk).wait_send()
        near_edge_copy(chunk).wait_send()

        @pl.when(jnp.logical_and(gives, chunk < direct))
        def _():
            relay_copy(chunk).wait_send()

        @pl.when(jnp.logical_and(gives, chunk < detours))
        def _():
            pass_on_copy(chunk).wait_send()

        @pl.when(jnp.logical_and(takes, chunk < detours))
        def _():
            pass_copy(chunk).wait_send()

        @pl.when(takes)
        def _():
            relay_edge_copy(chunk).wait_send()

        return carry

    lax.fori_loop(0, chunks, sent, 0)

    def far_sent(offset, carry):
        far_copy(offset).wait_send()
        return carry

    lax.fori_loop(1, blocks, far_sent, 0)


def fill_table(
    lists, lens, reach_time, reach_rows, spread, table, me, blocks, heads, per_source
):
    rows = spread.shape[1]
    tiles = lens.shape[1]
    spread[...] = jnp.zeros_like(spread)
    spread[0, :heads, :tiles] = lists[:, 0, :]
    spread[1, :heads, :tiles] = lists[:, 1, :]
    spread[2, :heads, :tiles] = lens[...]
    spread[3, :1, :heads] = reach_time[...]
    spread[4, :1, :heads] = reach_rows[...]
    one, two, count = spread[0], spread[1], spread[2]
    has_one, has_two = count > 0, count > 1
    none = jnp.int32(1 << 20)
    low = jnp.minimum(jnp.where(has_one, one, none), jnp.where(has_two, two, none))
    high = jnp.maximum(jnp.where(has_one, one, -1), jnp.where(has_two, two, -1))
    low = jnp.minimum(
        low, jnp.minimum(pltpu.roll(low, LANES - 1, 1), pltpu.roll(low, LANES - 2, 1))
    )
    high = jnp.maximum(
        high, jnp.maximum(pltpu.roll(high, LANES - 1, 1), pltpu.roll(high, LANES - 2, 1))
    )
    sub = lax.broadcasted_iota(jnp.int32, (rows, LANES), 0)
    lane = lax.broadcasted_iota(jnp.int32, (rows, LANES), 1)
    base = ROW_TILES * me
    mine = (low >= base) & (low < base + ROW_TILES)
    first = jnp.min(jnp.where(mine, sub, heads), axis=0, keepdims=True)
    first = jnp.where(first == heads, 0, first)
    last = jnp.max(jnp.where(mine, sub, 0), axis=0, keepdims=True)
    top_row = lax.broadcasted_iota(jnp.int32, (HEAD_ROW, LANES), 0)
    sends = jnp.zeros((HEAD_ROW, LANES), jnp.int32)
    for pair, pick in enumerate((first, last)[:per_source]):
        hit = (sub == pick) & mine
        low_tile = jnp.sum(jnp.where(hit, low - base, 0), axis=0, keepdims=True)
        high_tile = jnp.sum(jnp.where(hit, high - base, 0), axis=0, keepdims=True)
        for place, row in enumerate((pick, low_tile, high_tile)):
            sends = jnp.where(top_row == 3 * pair + place, row, sends)

    def column(matrix):
        return jnp.sum(matrix, axis=1, keepdims=True)

    def as_column(row):
        return column(jnp.where(sub == lane, row, 0))

    def as_row(values):
        return jnp.sum(jnp.where(sub == lane, values, 0), axis=0, keepdims=True)

    in_time, in_rows = spread[3, :1] > 0, spread[4, :1] > 0
    time_row = jnp.where(in_time, 1, 0)
    time_column = as_column(time_row)
    rows_column = as_column(jnp.where(in_rows, 1, 0))
    inside = lane < heads
    ahead = jnp.where(time_row > time_column, 1, 0) + jnp.where(
        (time_row == time_column) & (lane < sub), 1, 0
    )
    rank = column(jnp.where(inside, ahead, 0))
    order = jnp.sum(
        jnp.where((rank == lane) & (sub < heads), sub, 0), axis=0, keepdims=True
    )
    sends = jnp.where(top_row == ORDER_ROW, order, sends)
    table[:HEAD_ROW] = sends

    own_low = column(jnp.where(lane == base, low, 0))
    own_high = column(jnp.where(lane == base, high, 0))
    source = jnp.clip(own_low, 0, ROW_TILES * blocks) * 171 // 512
    planes = blocks // 4
    plane = me // 4 - source // 4
    plane = jnp.where(plane < 0, plane + planes, plane)
    flips = (me // 2 + source // 2) % 2
    offset = 4 * plane + 2 * flips + (me + source) % 2
    earlier = (as_row(source) == source) & (lane < sub) & inside
    slot = jnp.where(column(jnp.where(earlier, 1, 0)) > 0, LIST * (per_source - 1), 0)
    columns = [offset, slot, rank, time_column, rows_column, time_column * rows_column]
    for tile in range(ROW_TILES):
        for wanted in (own_low, own_high):
            found = (has_one & (one == wanted)) | (has_two & (two == wanted))
            columns.append(column(jnp.where(found & (lane == base + tile), 1, 0)))
    heads_table = jnp.zeros((rows, LANES), jnp.int32)
    for place, values in enumerate(columns):
        heads_table = jnp.where(lane == place, values, heads_table)
    table[HEAD_ROW:] = heads_table


def on_device(queries, keys, values, block_list, list_len, window_time, window_rows):
    tiles, tok, feat = queries.shape
    heads = window_time.shape[0]
    dim = feat // heads
    blocks = lax.axis_size("seq")
    per_source = (heads + blocks - 2) // (blocks - 1)
    meta = (
        jnp.transpose(block_list, (1, 2, 0)),
        jnp.transpose(list_len),
        window_time.reshape(1, heads),
        window_rows.reshape(1, heads),
    )
    steps = REACH_STEPS + (heads,)
    reaching = jnp.sum(jnp.where(window_time > 0, 1, 0))
    branch = jnp.right_shift(reaching - (REACH_STEPS[0] - 1), 1)
    calls = [
        functools.partial(attend, count, number, blocks, heads, per_source)
        for number, count in enumerate(steps)
    ]
    return lax.switch(branch, calls, *meta, queries, keys, values)


def attend(reaching, number, blocks, heads, per_source, *operands):
    queries, keys = operands[-3:-1]
    tiles, tok, feat = queries.shape
    dim = feat // heads
    chunk_heads = 4 if reaching == 20 else 2
    chunks = reaching // chunk_heads
    detours = 2 * chunks // 5
    kind = keys.dtype
    rows = (heads + 7) // 8 * 8
    vmem = pl.BlockSpec(memory_space=pltpu.VMEM)
    anywhere = pl.BlockSpec(memory_space=pl.ANY)
    dma = pltpu.SemaphoreType.DMA
    return pl.pallas_call(
        functools.partial(
            kernel, blocks, heads, tok, dim, per_source, chunk_heads, chunks, detours
        ),
        out_shape=jax.ShapeDtypeStruct(queries.shape, queries.dtype),
        in_specs=[vmem] * 4 + [anywhere] * 3,
        out_specs=vmem,
        scratch_shapes=[
            pltpu.VMEM((5, rows, LANES), jnp.int32),
            pltpu.VMEM((HEAD_ROW + rows, LANES), jnp.int32),
            pltpu.SMEM((HEAD_ROW + rows, LANES), jnp.int32),
            pltpu.VMEM((heads, tiles, tok, dim), kind),
            pltpu.VMEM((2, heads, tiles, tok, dim), kind),
            pltpu.VMEM((2, reaching, tiles, tok, dim), kind),
            pltpu.VMEM((2, heads, tok, dim), kind),
            pltpu.VMEM((2, detours * chunk_heads, tiles, tok, dim), kind),
            pltpu.VMEM((2, reaching, tiles, tok, dim), kind),
            pltpu.VMEM((2, reaching, tok, dim), kind),
            pltpu.VMEM((2, reaching, tiles, tok, dim), kind),
            pltpu.VMEM((2, reaching, tok, dim), kind),
            pltpu.VMEM((blocks, per_source * LIST, 2, tok, dim), kind),
            pltpu.VMEM((blocks, per_source * LIST, 2, tok, dim), kind),
            pltpu.VMEM((heads, tiles, tok, dim), jnp.float32),
            pltpu.VMEM((heads, tiles, tok, 1), jnp.float32),
            pltpu.VMEM((heads, tiles, tok, 1), jnp.float32),
            dma,
            dma((3, heads)),
            dma((2,)),
            dma((detours, 2)),
            dma((chunks, 2)),
            dma((chunks, 2)),
            dma((chunks, 2)),
            dma((chunks, 2)),
            dma((blocks, 2)),
        ],
        compiler_params=pltpu.CompilerParams(
            collective_id=number, has_side_effects=True, vmem_limit_bytes=56 * 1024 * 1024
        ),
        cost_estimate=pl.CostEstimate(
            flops=4 * heads * tiles * 10 * tok * tok * dim,
            bytes_accessed=4 * tiles * tok * feat * 2,
            transcendentals=heads * tiles * 10 * tok * tok,
        ),
    )(*operands)


def solution(mesh):
    return jax.shard_map(
        on_device,
        mesh=mesh,
        in_specs=(
            P(("group", "seq"), None, None),
            P(("group", "seq"), None, None),
            P(("group", "seq"), None, None),
            P("group", None, None),
            P("group", None),
            P(),
            P(),
        ),
        out_specs=P(("group", "seq"), None, None),
        check_vma=False,
    )
```

```python
import functools
import math

import jax
import jax.numpy as jnp
from jax import lax
from jax.experimental import pallas as pl
from jax.experimental.pallas import tpu as pltpu
from jax.sharding import PartitionSpec as P

ROW_TILES = 3
ROW_BLOCKS = 2
LIST = 2
REACH_STEPS = (8, 10, 12, 14)
BIG_NEG = -1e30
ORDER_ROW = 6
HEAD_ROW = 8
LANES = 128


def kernel(
    blocks, heads, tok, dim, per_source, chunk_heads, chunks, detours,
    lists, lens, reach_time, reach_rows, q_hbm, k_hbm, v_hbm, out_ref,
    spread, table, meta, qs, kv, packed, edge, passing, near, near_edge, relayed, relayed_edge, far_out, far_in, acc, top, total,
    meta_sem, load_sem, edge_sem, pass_sem, near_sem, near_edge_sem, relay_sem, relay_edge_sem, far_sem,
):
    me = lax.axis_index("seq")
    side = lax.rem(me, ROW_BLOCKS)
    time = me // ROW_BLOCKS
    times = blocks // ROW_BLOCKS
    odd = lax.rem(time, 2)
    partner = me + 1 - 2 * side
    mirror = me + ROW_BLOCKS * (1 - 2 * odd)
    ahead = 2 * (1 - 2 * odd)
    gives = jnp.logical_and(time + ahead >= 0, time + ahead < times)
    takes = jnp.logical_and(time - ahead >= 0, time - ahead < times)
    relay_to = me + ROW_BLOCKS * ahead
    edge_tile = 2 - 2 * side
    other_tile = 2 * side
    direct = chunks - detours

    def remote(src, dst, sems, device):
        return pltpu.make_async_remote_copy(
            src_ref=src, dst_ref=dst, send_sem=sems.at[0], recv_sem=sems.at[1],
            device_id={"seq": device}, device_id_type=pl.DeviceIdType.MESH,
        )

    def part_of(chunk):
        return pl.ds(chunk * chunk_heads, chunk_heads)

    def near_copy(chunk):
        part = part_of(chunk)
        return remote(packed.at[:, part], near.at[:, part], near_sem.at[chunk], mirror)

    def near_edge_copy(chunk):
        part = part_of(chunk)
        return remote(
            near.at[:, part, edge_tile], near_edge.at[:, part],
            near_edge_sem.at[chunk], partner,
        )

    def pass_copy(chunk):
        return remote(
            packed.at[:, part_of(direct + chunk)], passing.at[:, part_of(chunk)],
            pass_sem.at[chunk], me - ROW_BLOCKS * ahead,
        )

    def pass_on_copy(chunk):
        return remote(
            passing.at[:, part_of(chunk)], relayed.at[:, part_of(direct + chunk)],
            relay_sem.at[direct + chunk], mirror,
        )

    def relay_copy(chunk):
        part = part_of(chunk)
        return remote(
            near.at[:, part], relayed.at[:, part], relay_sem.at[chunk], relay_to
        )

    def relay_edge_copy(chunk):
        part = part_of(chunk)
        return remote(
            relayed.at[:, part, edge_tile], relayed_edge.at[:, part],
            relay_edge_sem.at[chunk], partner,
        )

    def far_target(offset):
        plane = lax.rem(me // 4 + offset // 4, blocks // 4)
        return 4 * plane + 2 * lax.rem(odd + offset // 2, 2) + lax.rem(side + offset, 2)

    def far_copy(offset):
        return remote(
            far_out.at[offset], far_in.at[offset], far_sem.at[offset], far_target(offset)
        )

    def loads(head):
        cols = pl.ds(pl.multiple_of(head * dim, dim), dim)
        return [
            pltpu.make_async_copy(array.at[:, :, cols], held, load_sem.at[which, head])
            for which, (array, held) in enumerate(
                ((k_hbm, kv.at[0, head]), (v_hbm, kv.at[1, head]), (q_hbm, qs.at[head]))
            )
        ]

    def start_loads(head, carry):
        for copy in loads(head):
            copy.start()
        return carry

    def end_loads(head, carry):
        for copy in loads(head):
            copy.wait()
        return carry

    lax.fori_loop(0, heads, start_loads, 0)
    fill_table(
        lists, lens, reach_time, reach_rows, spread, table, me, blocks, heads, per_source
    )
    copy_meta = pltpu.make_async_copy(table, meta, meta_sem)
    copy_meta.start()
    barrier = pltpu.get_barrier_semaphore()

    def greet(offset, carry):
        pl.semaphore_signal(
            barrier, inc=1, device_id={"seq": lax.rem(me + offset, blocks)},
            device_id_type=pl.DeviceIdType.MESH,
        )
        return carry

    lax.fori_loop(1, blocks, greet, 0)
    lax.fori_loop(0, heads, end_loads, 0)
    pl.semaphore_wait(barrier, blocks - 1)
    copy_meta.wait()

    edge_copy = remote(kv.at[:, :, edge_tile], edge, edge_sem, partner)
    edge_copy.start()

    def start_near(chunk, carry):
        near_copy(chunk).start()
        return carry

    def pack(index, carry):
        head = meta[ORDER_ROW, index]
        for part in range(2):
            for tile in range(ROW_TILES):
                packed[part, index, tile] = kv[part, head, tile]
        return carry

    lax.fori_loop(0, chunks * chunk_heads, pack, 0)

    @pl.when(takes)
    def _():
        for chunk in range(detours):
            pass_copy(chunk).start()

    lax.fori_loop(0, chunks, start_near, 0)

    def send_far(offset):
        target = far_target(offset)
        for pair in range(per_source):
            head = meta[3 * pair, ROW_TILES * target]
            for which in range(LIST):
                tile = meta[3 * pair + 1 + which, ROW_TILES * target]
                for part in range(2):
                    far_out[offset, pair * LIST + which, part] = kv[part, head, tile]
        far_copy(offset).start()

    def far_straight(place, carry):
        plane = lax.rem(place // 2 + blocks // 8, blocks // 4)
        offset = 4 * plane + lax.rem(place, 2)

        @pl.when(offset > 0)
        def _():
            send_far(offset)

        return carry

    def far_across(place, carry):
        plane = lax.rem(place // 2 + blocks // 8, blocks // 4)
        send_far(4 * plane + 2 + lax.rem(place, 2))
        return carry

    far_early, far_half = blocks // 8, blocks // 2
    lax.fori_loop(0, far_early, far_straight, 0)

    factor = math.log2(math.e) / math.sqrt(dim)

    def scores_of(query, key, bias):
        product = lax.dot_general(
            query, key, (((1,), (1,)), ((), ())), preferred_element_type=jnp.float32
        )
        return product * factor + bias

    def fold(head, tile, scores, value, first):
        high = jnp.max(scores, axis=1, keepdims=True)
        if not first:
            old = top[head, tile]
            high = jnp.maximum(high, old)
            shrink = jnp.exp2(old - high)
        weights = jnp.exp2(scores - high)
        amount = jnp.sum(weights, axis=1, keepdims=True)
        mixed = jnp.dot(
            weights.astype(jnp.bfloat16), value, preferred_element_type=jnp.float32
        )
        if not first:
            amount = amount + total[head, tile] * shrink
            mixed = mixed + acc[head, tile] * shrink
        return high, amount, mixed

    def keep(head, tile, state):
        top[head, tile], total[head, tile], acc[head, tile] = state

    def closed(head, column):
        return (meta[HEAD_ROW + head, column].astype(jnp.float32) - 1.0) * -BIG_NEG

    def window_row(index, rows, edges, own):
        head = meta[ORDER_ROW, index]
        spot = head if own else index
        along = jnp.float32(0.0) if own else closed(head, 3)
        lane = lax.broadcasted_iota(jnp.int32, (1, 3 * tok), 1)
        bias = jnp.where(lane < tok, along, closed(head, 4 if own else 5))
        k_mid, v_mid = rows[0, spot, 1], rows[1, spot, 1]
        k_edge, v_edge = rows[0, spot, edge_tile], rows[1, spot, edge_tile]
        k_other, v_other = rows[0, spot, other_tile], rows[1, spot, other_tile]
        k_out, v_out = edges[0, spot], edges[1, spot]
        for tile, key, value in (
            (1, (k_mid, k_edge, k_other), (v_mid, v_edge, v_other)),
            (edge_tile, (k_edge, k_mid, k_out), (v_edge, v_mid, v_out)),
            (other_tile, (k_other, k_mid), (v_other, v_mid)),
        ):
            key = jnp.concatenate(key, axis=0)
            value = jnp.concatenate(value, axis=0)
            scores = scores_of(qs[head, tile], key, bias[:, : key.shape[0]])
            keep(index, tile, fold(index, tile, scores, value, own))

    def own_row(head, carry):
        window_row(head, kv, edge, True)
        return carry


    def near_rows(chunk):
        def step(inner, carry):
            window_row(chunk * chunk_heads + inner, near, near_edge, False)
            return carry

        lax.fori_loop(0, chunk_heads, step, 0)

    def relayed_rows(chunk):
        def step(inner, carry):
            window_row(chunk * chunk_heads + inner, relayed, relayed_edge, False)
            return carry

        lax.fori_loop(0, chunk_heads, step, 0)

    def relay_arrived(chunk):
        relay_copy(chunk).wait_recv()
        relay_edge_copy(chunk).start()

    def relay_used(chunk):
        relay_edge_copy(chunk).wait_recv()
        relayed_rows(chunk)

    def time_chunk(chunk, carry):
        near_copy(chunk).wait_recv()
        near_edge_copy(chunk).start()

        @pl.when(jnp.logical_and(gives, chunk < direct))
        def _():
            relay_copy(chunk).start()

        @pl.when(jnp.logical_and(gives, chunk >= direct))
        def _():
            pass_copy(chunk - direct).wait_recv()
            pass_on_copy(chunk - direct).start()

        straight = [
            far_early + (far_half - far_early) * jnp.minimum(2 * step, chunks) // chunks
            for step in (chunk, chunk + 1)
        ]
        across = [
            far_half * jnp.maximum(2 * step - chunks, 0) // chunks for step in (chunk, chunk + 1)
        ]
        lax.fori_loop(*straight, far_straight, 0)
        lax.fori_loop(*across, far_across, 0)
        @pl.when(chunk == 0)
        def _():
            edge_copy.wait_recv()

        lax.fori_loop(chunk * heads // chunks, (chunk + 1) * heads // chunks, own_row, 0)
        near_edge_copy(chunk).wait_recv()
        near_rows(chunk)
        return carry

    lax.fori_loop(0, chunks, time_chunk, 0)

    def relayed_chunk(chunk, carry):
        relay_arrived(chunk)

        @pl.when(chunk > 0)
        def _():
            relay_used(chunk - 1)

        return carry

    @pl.when(takes)
    def _():
        lax.fori_loop(0, chunks, relayed_chunk, 0)
        relay_used(chunks - 1)

    def far_arrived(offset, carry):
        far_copy(offset).wait_recv()
        return carry

    lax.fori_loop(1, blocks, far_arrived, 0)

    def far_head(head, carry):
        cols = pl.ds(pl.multiple_of(head * dim, dim), dim)
        offset, slot = meta[HEAD_ROW + head, 0], meta[HEAD_ROW + head, 1]
        key = jnp.concatenate([far_in[offset, slot + w, 0] for w in range(LIST)], axis=0)
        value = jnp.concatenate([far_in[offset, slot + w, 1] for w in range(LIST)], axis=0)
        lane = lax.broadcasted_iota(jnp.int32, (1, LIST * tok), 1)
        for tile in range(ROW_TILES):
            bias = jnp.where(
                lane < tok, closed(head, 6 + 2 * tile), closed(head, 7 + 2 * tile)
            )
            scores = scores_of(qs[head, tile], key, bias)
            _, amount, mixed = fold(meta[HEAD_ROW + head, 2], tile, scores, value, False)
            out_ref[tile, :, cols] = (mixed / amount).astype(out_ref.dtype)
        return carry

    lax.fori_loop(0, heads, far_head, 0, unroll=2)

    edge_copy.wait_send()

    def sent(chunk, carry):
        near_copy(chunk).wait_send()
        near_edge_copy(chunk).wait_send()

        @pl.when(jnp.logical_and(gives, chunk < direct))
        def _():
            relay_copy(chunk).wait_send()

        @pl.when(jnp.logical_and(gives, chunk < detours))
        def _():
            pass_on_copy(chunk).wait_send()

        @pl.when(jnp.logical_and(takes, chunk < detours))
        def _():
            pass_copy(chunk).wait_send()

        @pl.when(takes)
        def _():
            relay_edge_copy(chunk).wait_send()

        return carry

    lax.fori_loop(0, chunks, sent, 0)

    def far_sent(offset, carry):
        far_copy(offset).wait_send()
        return carry

    lax.fori_loop(1, blocks, far_sent, 0)


def fill_table(
    lists, lens, reach_time, reach_rows, spread, table, me, blocks, heads, per_source
):
    rows = spread.shape[1]
    tiles = lens.shape[1]
    spread[...] = jnp.zeros_like(spread)
    spread[0, :heads, :tiles] = lists[:, 0, :]
    spread[1, :heads, :tiles] = lists[:, 1, :]
    spread[2, :heads, :tiles] = lens[...]
    spread[3, :1, :heads] = reach_time[...]
    spread[4, :1, :heads] = reach_rows[...]
    one, two, count = spread[0], spread[1], spread[2]
    has_one, has_two = count > 0, count > 1
    none = jnp.int32(1 << 20)
    low = jnp.minimum(jnp.where(has_one, one, none), jnp.where(has_two, two, none))
    high = jnp.maximum(jnp.where(has_one, one, -1), jnp.where(has_two, two, -1))
    low = jnp.minimum(
        low, jnp.minimum(pltpu.roll(low, LANES - 1, 1), pltpu.roll(low, LANES - 2, 1))
    )
    high = jnp.maximum(
        high, jnp.maximum(pltpu.roll(high, LANES - 1, 1), pltpu.roll(high, LANES - 2, 1))
    )
    sub = lax.broadcasted_iota(jnp.int32, (rows, LANES), 0)
    lane = lax.broadcasted_iota(jnp.int32, (rows, LANES), 1)
    base = ROW_TILES * me
    mine = (low >= base) & (low < base + ROW_TILES)
    first = jnp.min(jnp.where(mine, sub, heads), axis=0, keepdims=True)
    first = jnp.where(first == heads, 0, first)
    last = jnp.max(jnp.where(mine, sub, 0), axis=0, keepdims=True)
    top_row = lax.broadcasted_iota(jnp.int32, (HEAD_ROW, LANES), 0)
    sends = jnp.zeros((HEAD_ROW, LANES), jnp.int32)
    for pair, pick in enumerate((first, last)[:per_source]):
        hit = (sub == pick) & mine
        low_tile = jnp.sum(jnp.where(hit, low - base, 0), axis=0, keepdims=True)
        high_tile = jnp.sum(jnp.where(hit, high - base, 0), axis=0, keepdims=True)
        for place, row in enumerate((pick, low_tile, high_tile)):
            sends = jnp.where(top_row == 3 * pair + place, row, sends)

    def column(matrix):
        return jnp.sum(matrix, axis=1, keepdims=True)

    def as_column(row):
        return column(jnp.where(sub == lane, row, 0))

    def as_row(values):
        return jnp.sum(jnp.where(sub == lane, values, 0), axis=0, keepdims=True)

    in_time, in_rows = spread[3, :1] > 0, spread[4, :1] > 0
    time_row = jnp.where(in_time, 1, 0)
    time_column = as_column(time_row)
    rows_column = as_column(jnp.where(in_rows, 1, 0))
    inside = lane < heads
    ahead = jnp.where(time_row > time_column, 1, 0) + jnp.where(
        (time_row == time_column) & (lane < sub), 1, 0
    )
    rank = column(jnp.where(inside, ahead, 0))
    order = jnp.sum(
        jnp.where((rank == lane) & (sub < heads), sub, 0), axis=0, keepdims=True
    )
    sends = jnp.where(top_row == ORDER_ROW, order, sends)
    table[:HEAD_ROW] = sends

    own_low = column(jnp.where(lane == base, low, 0))
    own_high = column(jnp.where(lane == base, high, 0))
    source = jnp.clip(own_low, 0, ROW_TILES * blocks) * 171 // 512
    planes = blocks // 4
    plane = me // 4 - source // 4
    plane = jnp.where(plane < 0, plane + planes, plane)
    flips = (me // 2 + source // 2) % 2
    offset = 4 * plane + 2 * flips + (me + source) % 2
    earlier = (as_row(source) == source) & (lane < sub) & inside
    slot = jnp.where(column(jnp.where(earlier, 1, 0)) > 0, LIST * (per_source - 1), 0)
    columns = [offset, slot, rank, time_column, rows_column, time_column * rows_column]
    for tile in range(ROW_TILES):
        for wanted in (own_low, own_high):
            found = (has_one & (one == wanted)) | (has_two & (two == wanted))
            columns.append(column(jnp.where(found & (lane == base + tile), 1, 0)))
    heads_table = jnp.zeros((rows, LANES), jnp.int32)
    for place, values in enumerate(columns):
        heads_table = jnp.where(lane == place, values, heads_table)
    table[HEAD_ROW:] = heads_table


def on_device(queries, keys, values, block_list, list_len, window_time, window_rows):
    tiles, tok, feat = queries.shape
    heads = window_time.shape[0]
    dim = feat // heads
    blocks = lax.axis_size("seq")
    per_source = (heads + blocks - 2) // (blocks - 1)
    meta = (
        jnp.transpose(block_list, (1, 2, 0)),
        jnp.transpose(list_len),
        window_time.reshape(1, heads),
        window_rows.reshape(1, heads),
    )
    steps = REACH_STEPS + (heads,)
    reaching = jnp.sum(jnp.where(window_time > 0, 1, 0))
    branch = jnp.right_shift(reaching - (REACH_STEPS[0] - 1), 1)
    calls = [
        functools.partial(attend, count, number, blocks, heads, per_source)
        for number, count in enumerate(steps)
    ]
    return lax.switch(branch, calls, *meta, queries, keys, values)


def attend(reaching, number, blocks, heads, per_source, *operands):
    queries, keys = operands[-3:-1]
    tiles, tok, feat = queries.shape
    dim = feat // heads
    chunk_heads = 4 if reaching == 20 else 2
    chunks = reaching // chunk_heads
    detours = 2 * chunks // 5
    kind = keys.dtype
    rows = (heads + 7) // 8 * 8
    vmem = pl.BlockSpec(memory_space=pltpu.VMEM)
    anywhere = pl.BlockSpec(memory_space=pl.ANY)
    dma = pltpu.SemaphoreType.DMA
    return pl.pallas_call(
        functools.partial(
            kernel, blocks, heads, tok, dim, per_source, chunk_heads, chunks, detours
        ),
        out_shape=jax.ShapeDtypeStruct(queries.shape, queries.dtype),
        in_specs=[vmem] * 4 + [anywhere] * 3,
        out_specs=vmem,
        scratch_shapes=[
            pltpu.VMEM((5, rows, LANES), jnp.int32),
            pltpu.VMEM((HEAD_ROW + rows, LANES), jnp.int32),
            pltpu.SMEM((HEAD_ROW + rows, LANES), jnp.int32),
            pltpu.VMEM((heads, tiles, tok, dim), kind),
            pltpu.VMEM((2, heads, tiles, tok, dim), kind),
            pltpu.VMEM((2, reaching, tiles, tok, dim), kind),
            pltpu.VMEM((2, heads, tok, dim), kind),
            pltpu.VMEM((2, detours * chunk_heads, tiles, tok, dim), kind),
            pltpu.VMEM((2, reaching, tiles, tok, dim), kind),
            pltpu.VMEM((2, reaching, tok, dim), kind),
            pltpu.VMEM((2, reaching, tiles, tok, dim), kind),
            pltpu.VMEM((2, reaching, tok, dim), kind),
            pltpu.VMEM((blocks, per_source * LIST, 2, tok, dim), kind),
            pltpu.VMEM((blocks, per_source * LIST, 2, tok, dim), kind),
            pltpu.VMEM((heads, tiles, tok, dim), jnp.float32),
            pltpu.VMEM((heads, tiles, tok, 1), jnp.float32),
            pltpu.VMEM((heads, tiles, tok, 1), jnp.float32),
            dma,
            dma((3, heads)),
            dma((2,)),
            dma((detours, 2)),
            dma((chunks, 2)),
            dma((chunks, 2)),
            dma((chunks, 2)),
            dma((chunks, 2)),
            dma((blocks, 2)),
        ],
        compiler_params=pltpu.CompilerParams(
            collective_id=number, has_side_effects=True, vmem_limit_bytes=56 * 1024 * 1024
        ),
        cost_estimate=pl.CostEstimate(
            flops=4 * heads * tiles * 10 * tok * tok * dim,
            bytes_accessed=4 * tiles * tok * feat * 2,
            transcendentals=heads * tiles * 10 * tok * tok,
        ),
    )(*operands)


def solution(mesh):
    return jax.shard_map(
        on_device,
        mesh=mesh,
        in_specs=(
            P(("group", "seq"), None, None),
            P(("group", "seq"), None, None),
            P(("group", "seq"), None, None),
            P("group", None, None),
            P("group", None),
            P(),
            P(),
        ),
        out_specs=P(("group", "seq"), None, None),
        check_vma=False,
    )
```

```python
import functools
import math

import jax
import jax.numpy as jnp
from jax import lax
from jax.experimental import pallas as pl
from jax.experimental.pallas import tpu as pltpu
from jax.sharding import PartitionSpec as P

ROW_TILES = 3
ROW_BLOCKS = 2
LIST = 2
REACH_STEPS = (8, 10, 12, 14)
BIG_NEG = -1e30
ORDER_ROW = 6
HEAD_ROW = 8
LANES = 128


def kernel(
    blocks, heads, tok, dim, per_source, chunk_heads, chunks, detours,
    lists, lens, reach_time, reach_rows, q_hbm, k_hbm, v_hbm, out_ref,
    spread, table, meta, qs, kv, packed, edge, passing, near, near_edge, relayed, relayed_edge, far_out, far_in, acc, top, total,
    meta_sem, load_sem, edge_sem, pass_sem, near_sem, near_edge_sem, relay_sem, relay_edge_sem, far_sem,
):
    me = lax.axis_index("seq")
    side = lax.rem(me, ROW_BLOCKS)
    time = me // ROW_BLOCKS
    times = blocks // ROW_BLOCKS
    odd = lax.rem(time, 2)
    partner = me + 1 - 2 * side
    mirror = me + ROW_BLOCKS * (1 - 2 * odd)
    ahead = 2 * (1 - 2 * odd)
    gives = jnp.logical_and(time + ahead >= 0, time + ahead < times)
    takes = jnp.logical_and(time - ahead >= 0, time - ahead < times)
    relay_to = me + ROW_BLOCKS * ahead
    edge_tile = 2 - 2 * side
    other_tile = 2 * side
    direct = chunks - detours

    def remote(src, dst, sems, device):
        return pltpu.make_async_remote_copy(
            src_ref=src, dst_ref=dst, send_sem=sems.at[0], recv_sem=sems.at[1],
            device_id={"seq": device}, device_id_type=pl.DeviceIdType.MESH,
        )

    def part_of(chunk):
        return pl.ds(chunk * chunk_heads, chunk_heads)

    def near_copy(chunk):
        part = part_of(chunk)
        return remote(packed.at[:, part], near.at[:, part], near_sem.at[chunk], mirror)

    def near_edge_copy(chunk):
        part = part_of(chunk)
        return remote(
            near.at[:, part, edge_tile], near_edge.at[:, part],
            near_edge_sem.at[chunk], partner,
        )

    def pass_copy(chunk):
        return remote(
            packed.at[:, part_of(direct + chunk)], passing.at[:, part_of(chunk)],
            pass_sem.at[chunk], me - ROW_BLOCKS * ahead,
        )

    def pass_on_copy(chunk):
        return remote(
            passing.at[:, part_of(chunk)], relayed.at[:, part_of(direct + chunk)],
            relay_sem.at[direct + chunk], mirror,
        )

    def relay_copy(chunk):
        part = part_of(chunk)
        return remote(
            near.at[:, part], relayed.at[:, part], relay_sem.at[chunk], relay_to
        )

    def relay_edge_copy(chunk):
        part = part_of(chunk)
        return remote(
            relayed.at[:, part, edge_tile], relayed_edge.at[:, part],
            relay_edge_sem.at[chunk], partner,
        )

    def far_target(offset):
        plane = lax.rem(me // 4 + offset // 4, blocks // 4)
        return 4 * plane + 2 * lax.rem(odd + offset // 2, 2) + lax.rem(side + offset, 2)

    def far_copy(offset):
        return remote(
            far_out.at[offset], far_in.at[offset], far_sem.at[offset], far_target(offset)
        )

    def loads(head):
        cols = pl.ds(pl.multiple_of(head * dim, dim), dim)
        return [
            pltpu.make_async_copy(array.at[:, :, cols], held, load_sem.at[which, head])
            for which, (array, held) in enumerate(
                ((k_hbm, kv.at[0, head]), (v_hbm, kv.at[1, head]), (q_hbm, qs.at[head]))
            )
        ]

    def start_loads(head, carry):
        for copy in loads(head):
            copy.start()
        return carry

    def end_loads(head, carry):
        for copy in loads(head):
            copy.wait()
        return carry

    lax.fori_loop(0, heads, start_loads, 0)
    fill_table(
        lists, lens, reach_time, reach_rows, spread, table, me, blocks, heads, per_source
    )
    copy_meta = pltpu.make_async_copy(table, meta, meta_sem)
    copy_meta.start()
    barrier = pltpu.get_barrier_semaphore()

    def greet(offset, carry):
        pl.semaphore_signal(
            barrier, inc=1, device_id={"seq": lax.rem(me + offset, blocks)},
            device_id_type=pl.DeviceIdType.MESH,
        )
        return carry

    lax.fori_loop(1, blocks, greet, 0)
    lax.fori_loop(0, heads, end_loads, 0)
    pl.semaphore_wait(barrier, blocks - 1)
    copy_meta.wait()

    edge_copy = remote(kv.at[:, :, edge_tile], edge, edge_sem, partner)
    edge_copy.start()

    def start_near(chunk, carry):
        near_copy(chunk).start()
        return carry

    def pack(index, carry):
        head = meta[ORDER_ROW, index]
        for part in range(2):
            for tile in range(ROW_TILES):
                packed[part, index, tile] = kv[part, head, tile]
        return carry

    lax.fori_loop(0, chunks * chunk_heads, pack, 0)

    @pl.when(takes)
    def _():
        for chunk in range(detours):
            pass_copy(chunk).start()

    lax.fori_loop(0, chunks, start_near, 0)

    def send_far(offset):
        target = far_target(offset)
        for pair in range(per_source):
            head = meta[3 * pair, ROW_TILES * target]
            for which in range(LIST):
                tile = meta[3 * pair + 1 + which, ROW_TILES * target]
                for part in range(2):
                    far_out[offset, pair * LIST + which, part] = kv[part, head, tile]
        far_copy(offset).start()

    def far_straight(place, carry):
        plane = lax.rem(place // 2 + blocks // 8, blocks // 4)
        offset = 4 * plane + lax.rem(place, 2)

        @pl.when(offset > 0)
        def _():
            send_far(offset)

        return carry

    def far_across(place, carry):
        plane = lax.rem(place // 2 + blocks // 8, blocks // 4)
        send_far(4 * plane + 2 + lax.rem(place, 2))
        return carry

    lax.fori_loop(0, blocks // 2, far_straight, 0)
    lax.fori_loop(0, blocks // 2, far_across, 0)

    factor = math.log2(math.e) / math.sqrt(dim)

    def scores_of(query, key, bias):
        product = lax.dot_general(
            query, key, (((1,), (1,)), ((), ())), preferred_element_type=jnp.float32
        )
        return product * factor + bias

    def fold(head, tile, scores, value, first):
        high = jnp.max(scores, axis=1, keepdims=True)
        if not first:
            old = top[head, tile]
            high = jnp.maximum(high, old)
            shrink = jnp.exp2(old - high)
        weights = jnp.exp2(scores - high)
        amount = jnp.sum(weights, axis=1, keepdims=True)
        mixed = jnp.dot(
            weights.astype(jnp.bfloat16), value, preferred_element_type=jnp.float32
        )
        if not first:
            amount = amount + total[head, tile] * shrink
            mixed = mixed + acc[head, tile] * shrink
        return high, amount, mixed

    def keep(head, tile, state):
        top[head, tile], total[head, tile], acc[head, tile] = state

    def closed(head, column):
        return (meta[HEAD_ROW + head, column].astype(jnp.float32) - 1.0) * -BIG_NEG

    def window_row(index, rows, edges, own):
        head = meta[ORDER_ROW, index]
        spot = head if own else index
        along = jnp.float32(0.0) if own else closed(head, 3)
        lane = lax.broadcasted_iota(jnp.int32, (1, 3 * tok), 1)
        bias = jnp.where(lane < tok, along, closed(head, 4 if own else 5))
        k_mid, v_mid = rows[0, spot, 1], rows[1, spot, 1]
        k_edge, v_edge = rows[0, spot, edge_tile], rows[1, spot, edge_tile]
        k_other, v_other = rows[0, spot, other_tile], rows[1, spot, other_tile]
        k_out, v_out = edges[0, spot], edges[1, spot]
        for tile, key, value in (
            (1, (k_mid, k_edge, k_other), (v_mid, v_edge, v_other)),
            (edge_tile, (k_edge, k_mid, k_out), (v_edge, v_mid, v_out)),
            (other_tile, (k_other, k_mid), (v_other, v_mid)),
        ):
            key = jnp.concatenate(key, axis=0)
            value = jnp.concatenate(value, axis=0)
            scores = scores_of(qs[head, tile], key, bias[:, : key.shape[0]])
            keep(index, tile, fold(index, tile, scores, value, own))

    def own_row(head, carry):
        window_row(head, kv, edge, True)
        return carry


    def near_rows(chunk):
        def step(inner, carry):
            window_row(chunk * chunk_heads + inner, near, near_edge, False)
            return carry

        lax.fori_loop(0, chunk_heads, step, 0)

    def relayed_rows(chunk):
        def step(inner, carry):
            window_row(chunk * chunk_heads + inner, relayed, relayed_edge, False)
            return carry

        lax.fori_loop(0, chunk_heads, step, 0)

    def relay_arrived(chunk):
        relay_copy(chunk).wait_recv()
        relay_edge_copy(chunk).start()

    def relay_used(chunk):
        relay_edge_copy(chunk).wait_recv()
        relayed_rows(chunk)

    def time_chunk(chunk, carry):
        near_copy(chunk).wait_recv()
        near_edge_copy(chunk).start()

        @pl.when(jnp.logical_and(gives, chunk < direct))
        def _():
            relay_copy(chunk).start()

        @pl.when(jnp.logical_and(gives, jnp.logical_and(chunk > 0, chunk <= detours)))
        def _():
            pass_copy(chunk - 1).wait_recv()
            pass_on_copy(chunk - 1).start()

        @pl.when(chunk == 0)
        def _():
            edge_copy.wait_recv()

        lax.fori_loop(chunk * heads // chunks, (chunk + 1) * heads // chunks, own_row, 0)
        near_edge_copy(chunk).wait_recv()
        near_rows(chunk)
        return carry

    lax.fori_loop(0, chunks, time_chunk, 0)

    def relayed_chunk(chunk, carry):
        relay_arrived(chunk)

        @pl.when(chunk > 0)
        def _():
            relay_used(chunk - 1)

        return carry

    @pl.when(takes)
    def _():
        lax.fori_loop(0, chunks, relayed_chunk, 0)
        relay_used(chunks - 1)

    def far_arrived(offset, carry):
        far_copy(offset).wait_recv()
        return carry

    lax.fori_loop(1, blocks, far_arrived, 0)

    def far_head(head, carry):
        cols = pl.ds(pl.multiple_of(head * dim, dim), dim)
        offset, slot = meta[HEAD_ROW + head, 0], meta[HEAD_ROW + head, 1]
        key = jnp.concatenate([far_in[offset, slot + w, 0] for w in range(LIST)], axis=0)
        value = jnp.concatenate([far_in[offset, slot + w, 1] for w in range(LIST)], axis=0)
        lane = lax.broadcasted_iota(jnp.int32, (1, LIST * tok), 1)
        for tile in range(ROW_TILES):
            bias = jnp.where(
                lane < tok, closed(head, 6 + 2 * tile), closed(head, 7 + 2 * tile)
            )
            scores = scores_of(qs[head, tile], key, bias)
            _, amount, mixed = fold(meta[HEAD_ROW + head, 2], tile, scores, value, False)
            out_ref[tile, :, cols] = (mixed / amount).astype(out_ref.dtype)
        return carry

    lax.fori_loop(0, heads, far_head, 0, unroll=2)

    edge_copy.wait_send()

    def sent(chunk, carry):
        near_copy(chunk).wait_send()
        near_edge_copy(chunk).wait_send()

        @pl.when(jnp.logical_and(gives, chunk < direct))
        def _():
            relay_copy(chunk).wait_send()

        @pl.when(jnp.logical_and(gives, chunk < detours))
        def _():
            pass_on_copy(chunk).wait_send()

        @pl.when(jnp.logical_and(takes, chunk < detours))
        def _():
            pass_copy(chunk).wait_send()

        @pl.when(takes)
        def _():
            relay_edge_copy(chunk).wait_send()

        return carry

    lax.fori_loop(0, chunks, sent, 0)

    def far_sent(offset, carry):
        far_copy(offset).wait_send()
        return carry

    lax.fori_loop(1, blocks, far_sent, 0)


def fill_table(
    lists, lens, reach_time, reach_rows, spread, table, me, blocks, heads, per_source
):
    rows = spread.shape[1]
    tiles = lens.shape[1]
    spread[...] = jnp.zeros_like(spread)
    spread[0, :heads, :tiles] = lists[:, 0, :]
    spread[1, :heads, :tiles] = lists[:, 1, :]
    spread[2, :heads, :tiles] = lens[...]
    spread[3, :1, :heads] = reach_time[...]
    spread[4, :1, :heads] = reach_rows[...]
    one, two, count = spread[0], spread[1], spread[2]
    has_one, has_two = count > 0, count > 1
    none = jnp.int32(1 << 20)
    low = jnp.minimum(jnp.where(has_one, one, none), jnp.where(has_two, two, none))
    high = jnp.maximum(jnp.where(has_one, one, -1), jnp.where(has_two, two, -1))
    low = jnp.minimum(
        low, jnp.minimum(pltpu.roll(low, LANES - 1, 1), pltpu.roll(low, LANES - 2, 1))
    )
    high = jnp.maximum(
        high, jnp.maximum(pltpu.roll(high, LANES - 1, 1), pltpu.roll(high, LANES - 2, 1))
    )
    sub = lax.broadcasted_iota(jnp.int32, (rows, LANES), 0)
    lane = lax.broadcasted_iota(jnp.int32, (rows, LANES), 1)
    base = ROW_TILES * me
    mine = (low >= base) & (low < base + ROW_TILES)
    first = jnp.min(jnp.where(mine, sub, heads), axis=0, keepdims=True)
    first = jnp.where(first == heads, 0, first)
    last = jnp.max(jnp.where(mine, sub, 0), axis=0, keepdims=True)
    top_row = lax.broadcasted_iota(jnp.int32, (HEAD_ROW, LANES), 0)
    sends = jnp.zeros((HEAD_ROW, LANES), jnp.int32)
    for pair, pick in enumerate((first, last)[:per_source]):
        hit = (sub == pick) & mine
        low_tile = jnp.sum(jnp.where(hit, low - base, 0), axis=0, keepdims=True)
        high_tile = jnp.sum(jnp.where(hit, high - base, 0), axis=0, keepdims=True)
        for place, row in enumerate((pick, low_tile, high_tile)):
            sends = jnp.where(top_row == 3 * pair + place, row, sends)

    def column(matrix):
        return jnp.sum(matrix, axis=1, keepdims=True)

    def as_column(row):
        return column(jnp.where(sub == lane, row, 0))

    def as_row(values):
        return jnp.sum(jnp.where(sub == lane, values, 0), axis=0, keepdims=True)

    in_time, in_rows = spread[3, :1] > 0, spread[4, :1] > 0
    time_row = jnp.where(in_time, 1, 0)
    time_column = as_column(time_row)
    rows_column = as_column(jnp.where(in_rows, 1, 0))
    inside = lane < heads
    ahead = jnp.where(time_row > time_column, 1, 0) + jnp.where(
        (time_row == time_column) & (lane < sub), 1, 0
    )
    rank = column(jnp.where(inside, ahead, 0))
    order = jnp.sum(
        jnp.where((rank == lane) & (sub < heads), sub, 0), axis=0, keepdims=True
    )
    sends = jnp.where(top_row == ORDER_ROW, order, sends)
    table[:HEAD_ROW] = sends

    own_low = column(jnp.where(lane == base, low, 0))
    own_high = column(jnp.where(lane == base, high, 0))
    source = jnp.clip(own_low, 0, ROW_TILES * blocks) * 171 // 512
    planes = blocks // 4
    plane = me // 4 - source // 4
    plane = jnp.where(plane < 0, plane + planes, plane)
    flips = (me // 2 + source // 2) % 2
    offset = 4 * plane + 2 * flips + (me + source) % 2
    earlier = (as_row(source) == source) & (lane < sub) & inside
    slot = jnp.where(column(jnp.where(earlier, 1, 0)) > 0, LIST * (per_source - 1), 0)
    columns = [offset, slot, rank, time_column, rows_column, time_column * rows_column]
    for tile in range(ROW_TILES):
        for wanted in (own_low, own_high):
            found = (has_one & (one == wanted)) | (has_two & (two == wanted))
            columns.append(column(jnp.where(found & (lane == base + tile), 1, 0)))
    heads_table = jnp.zeros((rows, LANES), jnp.int32)
    for place, values in enumerate(columns):
        heads_table = jnp.where(lane == place, values, heads_table)
    table[HEAD_ROW:] = heads_table


def on_device(queries, keys, values, block_list, list_len, window_time, window_rows):
    tiles, tok, feat = queries.shape
    heads = window_time.shape[0]
    dim = feat // heads
    blocks = lax.axis_size("seq")
    per_source = (heads + blocks - 2) // (blocks - 1)
    meta = (
        jnp.transpose(block_list, (1, 2, 0)),
        jnp.transpose(list_len),
        window_time.reshape(1, heads),
        window_rows.reshape(1, heads),
    )
    steps = REACH_STEPS + (heads,)
    reaching = jnp.sum(jnp.where(window_time > 0, 1, 0))
    branch = jnp.right_shift(reaching - (REACH_STEPS[0] - 1), 1)
    calls = [
        functools.partial(attend, count, number, blocks, heads, per_source)
        for number, count in enumerate(steps)
    ]
    return lax.switch(branch, calls, *meta, queries, keys, values)


def attend(reaching, number, blocks, heads, per_source, *operands):
    queries, keys = operands[-3:-1]
    tiles, tok, feat = queries.shape
    dim = feat // heads
    chunk_heads = 4 if reaching == 20 else 2
    chunks = reaching // chunk_heads
    detours = 2 * chunks // 5
    kind = keys.dtype
    rows = (heads + 7) // 8 * 8
    vmem = pl.BlockSpec(memory_space=pltpu.VMEM)
    anywhere = pl.BlockSpec(memory_space=pl.ANY)
    dma = pltpu.SemaphoreType.DMA
    return pl.pallas_call(
        functools.partial(
            kernel, blocks, heads, tok, dim, per_source, chunk_heads, chunks, detours
        ),
        out_shape=jax.ShapeDtypeStruct(queries.shape, queries.dtype),
        in_specs=[vmem] * 4 + [anywhere] * 3,
        out_specs=vmem,
        scratch_shapes=[
            pltpu.VMEM((5, rows, LANES), jnp.int32),
            pltpu.VMEM((HEAD_ROW + rows, LANES), jnp.int32),
            pltpu.SMEM((HEAD_ROW + rows, LANES), jnp.int32),
            pltpu.VMEM((heads, tiles, tok, dim), kind),
            pltpu.VMEM((2, heads, tiles, tok, dim), kind),
            pltpu.VMEM((2, reaching, tiles, tok, dim), kind),
            pltpu.VMEM((2, heads, tok, dim), kind),
            pltpu.VMEM((2, detours * chunk_heads, tiles, tok, dim), kind),
            pltpu.VMEM((2, reaching, tiles, tok, dim), kind),
            pltpu.VMEM((2, reaching, tok, dim), kind),
            pltpu.VMEM((2, reaching, tiles, tok, dim), kind),
            pltpu.VMEM((2, reaching, tok, dim), kind),
            pltpu.VMEM((blocks, per_source * LIST, 2, tok, dim), kind),
            pltpu.VMEM((blocks, per_source * LIST, 2, tok, dim), kind),
            pltpu.VMEM((heads, tiles, tok, dim), jnp.float32),
            pltpu.VMEM((heads, tiles, tok, 1), jnp.float32),
            pltpu.VMEM((heads, tiles, tok, 1), jnp.float32),
            dma,
            dma((3, heads)),
            dma((2,)),
            dma((detours, 2)),
            dma((chunks, 2)),
            dma((chunks, 2)),
            dma((chunks, 2)),
            dma((chunks, 2)),
            dma((blocks, 2)),
        ],
        compiler_params=pltpu.CompilerParams(
            collective_id=number, has_side_effects=True, vmem_limit_bytes=56 * 1024 * 1024
        ),
        cost_estimate=pl.CostEstimate(
            flops=4 * heads * tiles * 10 * tok * tok * dim,
            bytes_accessed=4 * tiles * tok * feat * 2,
            transcendentals=heads * tiles * 10 * tok * tok,
        ),
    )(*operands)


def solution(mesh):
    return jax.shard_map(
        on_device,
        mesh=mesh,
        in_specs=(
            P(("group", "seq"), None, None),
            P(("group", "seq"), None, None),
            P(("group", "seq"), None, None),
            P("group", None, None),
            P("group", None),
            P(),
            P(),
        ),
        out_specs=P(("group", "seq"), None, None),
        check_vma=False,
    )
```
